512 devices in a mesh: dp: 8 (over y, x_hi), expert: 64 (over z, x_lo, core).
Axes of the slice: x: 4 (x_hi: 2, x_lo: 2; x = x_hi * 2 + x_lo), y: 4, z: 16, core: 2. Of those that a mesh axis runs over, the one named last changes fastest.
Arguments:
- tokens: bfloat16 [65536, 2048], P(('dp', 'expert')), may hold values from -6 to 6
- expert_ids: int32 [65536, 8], P(('dp', 'expert')), may hold values from 0 to 63, all different within a row; in each aligned block of 128 rows (0 to 127, 128 to 255, ...) at most 18 rows name the same one
- keep_mask: int32 [65536, 8], P(('dp', 'expert')), may hold values 0 or 1
- gate_weights: bfloat16 [65536, 8], P(('dp', 'expert')), may hold values from 0.049804688 to 0.5
- hidden_grad: bfloat16 [8, 64, 1152, 384], P('dp', 'expert'), may hold values from -4 to 4
- gate_pre: bfloat16 [8, 64, 1152, 384], P('dp', 'expert'), may hold values from -8 to 8
- up_pre: bfloat16 [8, 64, 1152, 384], P('dp', 'expert'), may hold values from -6 to 6
- gate_proj: bfloat16 [64, 2048, 384], P('expert', 'dp'), may hold values from -0.3125 to 0.3125
- up_proj: bfloat16 [64, 2048, 384], P('expert', 'dp'), may hold values from -0.3125 to 0.3125
Outputs:
- token_grad: bfloat16 [65536, 2048], P(('dp', 'expert'))
- gate_proj_grad: bfloat16 [64, 2048, 384], P('expert', 'dp')
- up_proj_grad: bfloat16 [64, 2048, 384], P('expert', 'dp')
The draws below stay inside these ranges and needn't reach their ends.
Inputs may be any that keep to these rules, and one draw needn't show every extreme that they name: `expert_ids`: among the 8 experts of one token none repeats; among the pairs of the 128 tokens of one device no expert is named more than 18 times, a bound that some block reaches.
All inputs are finite; a program needn't handle non-finite values. No bound on the sum of `keep_mask` on one device may be relied on, other than what follows from the above.
Results may differ from the reference program's by a relative error of at most 0.015.
Values may be sent and summed in bfloat16 or wider, within the bound.
A program may use at most 128 MiB of HBM per device.

```python
import math
import jax
import jax.numpy as jnp
import numpy as np
from jax import lax

D = 2048
FF_WIN = 384
K = 8
TOK_DEV = 128
EXPERTS = 64
CAP = 18
TOKENS = 65536
N_DP = 8
N_EXPERT = 64


def touch_ends(values, stream_key, smallest, high):
    place = [jax.random.randint(jax.random.fold_in(stream_key, axis), (), 0, length) for axis, length in enumerate(values.shape)]
    main_axis = values.shape.index(max(values.shape))
    beside = place[:main_axis] + [(place[main_axis] + 1) % values.shape[main_axis]] + place[main_axis + 1:]
    return values.at[tuple(place)].set(smallest).at[tuple(beside)].set(high)


def shard_levels(key, extent, split, smallest, largest):
    def one(position, blocks):
        draws = jax.random.uniform(jax.random.fold_in(jax.random.fold_in(key, 6), position), (blocks,), jnp.float32, smallest / len(split), largest / len(split))
        return jnp.repeat(jnp.exp(draws), extent[position] // blocks).reshape((-1,) + (1,) * (len(extent) - position - 1))

    gain = one(*split[0])
    for cut in split[1:]:
        gain = gain * one(*cut)
    return gain


def deal_out(key, own, number, rows, amount, top, reach, slope):
    sequence = jax.random.permutation(key, amount)
    crowded, usual = load_shares(amount, rows * top, reach, slope, True), load_shares(amount, rows * top, reach, slope, False)
    places = jnp.arange(amount)

    def named(lengths, offset_by):
        used = int((lengths > 0).sum())
        fixed = max(1, used // 4)
        passed = fixed + (places - fixed + offset_by * (used - fixed)) % max(1, amount - fixed)
        return jnp.zeros((amount,), jnp.int32).at[sequence[jnp.where(places < fixed, places, passed)]].set(jnp.asarray(lengths, jnp.int32))

    lengths = jnp.where(number % 4 == 0, named(crowded, number // 4), named(usual, number - number // 4 - 1))
    mixed = jax.random.permutation(jax.random.fold_in(own, 3), amount)
    donor, taker = mixed[0:amount // 2 * 2:2], mixed[1:amount // 2 * 2:2]
    slack = jnp.minimum(lengths[donor] - 1, reach - lengths[taker]) // 2
    slack = jnp.where((donor == sequence[0]) | (taker == sequence[0]) | (lengths[taker] == 0), 0, jnp.maximum(slack, 0))
    passed = jax.random.randint(jax.random.fold_in(own, 4), (amount // 2,), 0, 1 << 20) % (slack + 1)
    lengths = lengths.at[donor].add(-passed).at[taker].add(passed)
    items = jnp.searchsorted(jnp.cumsum(lengths), jnp.arange(rows * top), side="right").astype(jnp.int32)
    listing = items.reshape(top, rows).T
    listing = listing[jax.random.permutation(jax.random.fold_in(own, 1), rows)]
    offset_by = jax.random.randint(jax.random.fold_in(own, 2), (rows, 1), 0, top)
    return jnp.take_along_axis(listing, (jnp.arange(top)[None, :] + offset_by) % top, axis=1)


def load_shares(count, total, reach, slope, full):
    weights = [(1 << 20) // math.isqrt(standing ** slope) + 1 for standing in range(1, count + 1)]
    largest = reach if full else min(reach, max(-(-total // count), total * weights[0] // sum(weights)))
    least = 1 if total - largest >= count - 1 else 0
    holding, rest = [largest] + [least] * (count - 1), total - largest - least * (count - 1)
    while rest > 0:
        candidates = [i for i in range(1, count) if holding[i] < largest] or [i for i in range(1, count) if holding[i] < reach]
        whole, remaining = sum([weights[i] for i in candidates]), rest
        for i in candidates:
            extra = min(reach - holding[i], max(1, remaining * weights[i] // whole), rest)
            holding[i] = holding[i] + extra
            rest = rest - extra
    return np.array(holding)


def noise(stream_key, shape, scale, reach, pieces=(), kind=jnp.bfloat16):
    gain = shard_levels(stream_key, shape, pieces, -0.22, 0.18) if pieces else 1.0
    result = jax.random.normal(stream_key, shape, jnp.float32) * scale * gain
    return jnp.minimum(jnp.maximum(result, -reach), reach).astype(kind)


def setup_inputs(seed: int = 0) -> dict:
    arg_keys = jax.random.split(jax.random.key(seed), 10)
    tokens = noise(arg_keys[0], (TOKENS, D), 1.0, 6.0, ((0, 512),))
    expert_ids_keys = jax.random.split(jax.random.fold_in(arg_keys[1], 1), TOKENS // TOK_DEV)
    expert_ids_turns = jax.random.permutation(jax.random.fold_in(arg_keys[1], 3), TOKENS // TOK_DEV)
    expert_ids = jax.vmap(lambda own, number: deal_out(jax.random.fold_in(arg_keys[1], 2), own, number, TOK_DEV, EXPERTS, K, CAP, 2))(expert_ids_keys, expert_ids_turns).reshape((TOKENS, K))
    keep_mask = touch_ends((jax.random.randint(arg_keys[2], (TOKENS, K), 0, 16) < 15).astype(jnp.int32), jax.random.fold_in(arg_keys[2], 1), 0, 1)
    gate_weights = jnp.clip(jnp.exp(math.log(0.5) - 2.306499 * jax.random.uniform(arg_keys[3], (TOKENS, K), jnp.float32) ** shard_levels(arg_keys[3], (TOKENS, K), ((0, 512),), -0.2, 0.2)), 0.049804688, 0.5).astype(jnp.bfloat16)
    hidden_grad = noise(arg_keys[4], (N_DP, EXPERTS, N_EXPERT * CAP, FF_WIN), 0.5, 4.0, ((0, 8), (1, 64)))
    gate_pre = noise(arg_keys[5], (N_DP, EXPERTS, N_EXPERT * CAP, FF_WIN), 1.5, 8.0, ((0, 8), (1, 64)))
    up_pre = noise(arg_keys[6], (N_DP, EXPERTS, N_EXPERT * CAP, FF_WIN), 1.0, 6.0, ((0, 8), (1, 64)))
    gate_proj = noise(arg_keys[7], (EXPERTS, D, FF_WIN), FF_WIN ** -0.5, 0.3125, ((0, 64), (1, 8)))
    up_proj = noise(arg_keys[8], (EXPERTS, D, FF_WIN), FF_WIN ** -0.5, 0.3125, ((0, 64), (1, 8)))
    return {"tokens": tokens, "expert_ids": expert_ids, "keep_mask": keep_mask, "gate_weights": gate_weights, "hidden_grad": hidden_grad, "gate_pre": gate_pre, "up_pre": up_pre, "gate_proj": gate_proj, "up_proj": up_proj}


def slot_numbers(route_ids, kept):
    onehot = (route_ids[..., None] == jnp.arange(EXPERTS, dtype=jnp.int32)).astype(jnp.int32) * kept[..., None]
    before = jnp.cumsum(onehot, axis=1) - onehot
    return jnp.sum(before * onehot, axis=2).astype(jnp.int32)


def expert_pass(operands):
    inputs_rx, gates_rx, grad_hidden, pre_gate, pre_up, weight_gate, weight_up = operands
    pre_a = pre_gate.astype(jnp.float32)
    pre_b = pre_up.astype(jnp.float32)
    sigmoid_a = 1.0 / (1.0 + jnp.exp(-pre_a))
    scaled = gates_rx.astype(jnp.float32)[:, None] * grad_hidden.astype(jnp.float32)
    gate_delta = (scaled * pre_b * sigmoid_a * (1.0 + pre_a * (1.0 - sigmoid_a))).astype(jnp.bfloat16)
    up_delta = (scaled * pre_a * sigmoid_a).astype(jnp.bfloat16)
    slot_grad = jnp.dot(gate_delta, weight_gate.T, preferred_element_type=jnp.float32)
    slot_grad = (slot_grad + jnp.dot(up_delta, weight_up.T, preferred_element_type=jnp.float32)).astype(jnp.bfloat16)
    part_gate = jnp.dot(inputs_rx.T, gate_delta, preferred_element_type=jnp.float32).astype(jnp.bfloat16)
    part_up = jnp.dot(inputs_rx.T, up_delta, preferred_element_type=jnp.float32).astype(jnp.bfloat16)
    return slot_grad, part_gate, part_up


def reference(tokens, expert_ids, keep_mask, gate_weights, hidden_grad, gate_pre, up_pre, gate_proj, up_proj):
    group_tokens = N_EXPERT * TOK_DEV
    entries = group_tokens * K
    slot_rows = N_EXPERT * CAP
    route_ids = expert_ids.reshape(N_DP, N_EXPERT, TOK_DEV * K).astype(jnp.int32)
    kept = keep_mask.reshape(N_DP, N_EXPERT, TOK_DEV * K).astype(jnp.int32)
    total_gate = jnp.zeros((EXPERTS, D, FF_WIN), jnp.float32)
    total_up = jnp.zeros((EXPERTS, D, FF_WIN), jnp.float32)
    results = []
    source = (jnp.arange(N_EXPERT, dtype=jnp.int32) * CAP)[:, None]
    for group in range(N_DP):
        ids_here = route_ids[group]
        kept_here = kept[group]
        slot = slot_numbers(ids_here, kept_here)
        target = jnp.where(kept_here > 0, ids_here * slot_rows + source + slot, EXPERTS * slot_rows).reshape(-1).astype(jnp.int32)
        owner = jnp.full((EXPERTS * slot_rows,), entries, jnp.int32).at[target].set(jnp.arange(entries, dtype=jnp.int32), mode="drop")
        rows_here = tokens[group * group_tokens:(group + 1) * group_tokens]
        padded_rows = jnp.concatenate([rows_here, jnp.zeros((1, D), jnp.bfloat16)], axis=0)
        inputs_rx = padded_rows[owner // K].reshape(EXPERTS, slot_rows, D)
        weights_here = gate_weights[group * group_tokens:(group + 1) * group_tokens].reshape(-1)
        padded_weights = jnp.concatenate([weights_here, jnp.zeros((1,), jnp.bfloat16)])
        gates_rx = padded_weights[owner].reshape(EXPERTS, slot_rows)
        slot_grad, part_gate, part_up = lax.map(expert_pass, (inputs_rx, gates_rx, hidden_grad[group], gate_pre[group], up_pre[group], gate_proj, up_proj))
        total_gate = total_gate + part_gate.astype(jnp.float32)
        total_up = total_up + part_up.astype(jnp.float32)
        padded_grad = jnp.concatenate([slot_grad.reshape(EXPERTS * slot_rows, D), jnp.zeros((1, D), jnp.bfloat16)], axis=0)
        picked = padded_grad[target].reshape(group_tokens, K, D).astype(jnp.float32)
        results.append(jnp.sum(picked, axis=1).astype(jnp.bfloat16))
    token_grad = jnp.concatenate(results, axis=0)
    return token_grad, total_gate.astype(jnp.bfloat16), total_up.astype(jnp.bfloat16)
```

```python
import functools

import jax
import jax.numpy as jnp
from jax import lax
from jax.experimental import pallas as pl
from jax.experimental.pallas import tpu as pltpu
from jax.sharding import PartitionSpec as P

MESH = pl.DeviceIdType.MESH
BF = jnp.bfloat16
F32 = jnp.float32
I32 = jnp.int32
PLANE = 4


def mm_nt(a, b):
    return lax.dot_general(a, b, (((1,), (1,)), ((), ())), preferred_element_type=F32)


def mm(a, b):
    return jnp.dot(a, b, preferred_element_type=F32)


def flip(bit, by):
    return bit + by - 2 * bit * by


def kernel(
    nz, ny, cap, topk,
    ids_in, keep_in, gate_in, tok, hid, pre_a, pre_b, w_gate, w_up,
    tok_out, gate_out, up_out,
    xcol, meta, delta, dperm, dturn, wall, st, xs_send, xs, g_send, g_all,
    fwd, bwd, tsum, part, prow, xsend, xrow,
    ag_s, ag_r, me_s, me_r, xd_s, xd_r, gd_s, gd_r, wx_s, wx_r, wy_s, wy_r,
    rs_s, rs_r, py_s, py_r, px_s, px_r,
):
    n2 = nz // 2
    tdev, width = tok.shape
    half = tdev // 2
    ff = w_gate.shape[1]
    rows = hid.shape[0]
    ch = n2 * cap
    db = w_gate.shape[0]
    nt = min(512, width)
    e_ix, d_ix = lax.axis_index("expert"), lax.axis_index("dp")
    z, q = e_ix // PLANE, e_ix % PLANE
    xl, co = q // 2, q % 2
    y, xh = d_ix // 2, d_ix % 2
    zup = (d_ix, lax.rem(z + 1, nz) * PLANE + q)
    zdn = (d_ix, lax.rem(z + nz - 1, nz) * PLANE + q)
    column = [flip(xl, r // 2) * 2 + flip(co, r % 2) for r in range(PLANE)]
    plane = [(d_ix, z * PLANE + column[r]) for r in range(PLANE)]
    ypeer = [(lax.rem(y + dy, ny) * 2 + xh, e_ix) for dy in range(ny)]
    xpeer = (y * 2 + (1 - xh), e_ix)

    def pos(off):
        if off == -n2 or off == n2:
            return nz - 1
        return 2 * off if off >= 0 else -2 * off - 1

    def send(src, dst, s, r, dev):
        return pltpu.make_async_remote_copy(
            src_ref=src, dst_ref=dst, send_sem=s, recv_sem=r, device_id=dev, device_id_type=MESH
        )

    def slot_half(p, h):
        return xcol.at[p // n2, pl.ds((p % n2) * tdev + h * half, half)]

    def ag_copy(way, d, h):
        sign = -1 if way == 0 else 1
        src = tok.at[pl.ds(h * half, half)] if d == 1 else slot_half(pos(sign * (d - 1)), h)
        ix = (way, d * 2 + h)
        return send(src, slot_half(pos(sign * d), h), ag_s.at[ix], ag_r.at[ix], zup if way == 0 else zdn)

    def me_copy(way, d):
        sign = -1 if way == 0 else 1
        ix = (way, d)
        return send(meta.at[pos(sign * (d - 1))], meta.at[pos(sign * d)], me_s.at[ix], me_r.at[ix], zup if way == 0 else zdn)

    def xd_copy(c, r):
        return send(xs_send.at[c, r - 1], xs.at[pl.ds((c * PLANE + r) * ch, ch)], xd_s.at[c, r], xd_r.at[c, r], plane[r])

    def gd_copy(c, r):
        return send(g_send.at[c, r - 1], g_all.at[c, pl.ds(r * ch, ch)], gd_s.at[c, r], gd_r.at[c, r], plane[r])

    def wblock(i):
        return wall.at[pl.ds(pl.multiple_of(i * db, db), db)]

    wx = send(wblock(d_ix), wblock(d_ix), wx_s, wx_r, xpeer)

    def wy_copy(dy, rel):
        i = y * 2 + flip(xh, rel)
        return send(wblock(i), wblock(i), wy_s.at[dy, rel], wy_r.at[dy, rel], ypeer[dy])

    def wy_wait(dy, rel):
        i = lax.rem(y + ny - dy, ny) * 2 + flip(xh, rel)
        send(wblock(i), wblock(i), wy_s.at[dy, rel], wy_r.at[dy, rel], ypeer[dy]).wait_recv()

    def rs_copy(way, d, h):
        buf = fwd if way == 0 else bwd
        ix = (way, d * 2 + h)
        return send(buf.at[d, h], buf.at[d - 1, h], rs_s.at[ix], rs_r.at[ix], zup if way == 0 else zdn)

    def py_copy(dy, rel):
        return send(part.at[dy, rel], prow.at[dy - 1, rel], py_s.at[dy, rel], py_r.at[dy, rel], ypeer[dy])

    px = send(xsend, xrow, px_s, px_r, xpeer)
    started = []

    def go(copy):
        copy.start()
        started.append(copy)

    barrier = pltpu.get_barrier_semaphore()
    partners = [zup, zdn, xpeer] + plane[1:] + ypeer[1:]
    for dev in partners:
        pl.semaphore_signal(barrier, inc=1, device_id=dev, device_id_type=MESH)

    experts = nz * PLANE
    ids, keep = ids_in[...], keep_in[...]
    e_iota = lax.broadcasted_iota(I32, (experts, tdev), 0)
    named = jnp.zeros((experts, tdev), F32)
    for k in range(topk):
        named += jnp.where((e_iota == ids[k:k + 1, :]) & (keep[k:k + 1, :] > 0), 1.0, 0.0)
    earlier = jnp.where(
        lax.broadcasted_iota(I32, (tdev, tdev), 0) < lax.broadcasted_iota(I32, (tdev, tdev), 1), 1.0, 0.0
    ).astype(BF)
    before = mm(named.astype(BF), earlier)
    for k in range(topk):
        mine = ids[k:k + 1, :]
        slot = jnp.sum(jnp.where(e_iota == mine, before, 0.0), axis=0, keepdims=True)
        row = mine.astype(F32) * float(cap) + slot
        meta[0, k:k + 1, :] = jnp.where(keep[k:k + 1, :] > 0, row, -4096.0)
    meta[0, topk:2 * topk, :] = gate_in[...]
    mine_w = pl.ds(pl.multiple_of(d_ix * db, db), db)
    wall[mine_w, 0:ff] = w_gate[...]
    wall[mine_w, ff:2 * ff] = w_up[...]

    pl.semaphore_wait(barrier, len(partners))

    def ag_has(way, d, h):
        return d < n2 or (d == n2 and h == way)

    def me_has(way, d):
        return d < n2 or (d == n2 and way == 0)

    for way in range(2):
        go(me_copy(way, 1))
    for h in range(2):
        for way in range(2):
            if ag_has(way, 1, h):
                go(ag_copy(way, 1, h))
    go(wx)
    for dy in range(1, ny):
        go(wy_copy(dy, 0))

    events = [(d, h) for d in range(1, n2) for h in range(2)] + [(n2, 0)]
    queue = list(events)

    def ag_event():
        if not queue:
            return
        d, h = queue.pop(0)
        for way in range(2):
            if h == 0 and me_has(way, d):
                me_copy(way, d).wait_recv()
                if me_has(way, d + 1):
                    go(me_copy(way, d + 1))
        for way in range(2):
            hh = way if d == n2 else h
            ag_copy(way, d, hh).wait_recv()
            if ag_has(way, d + 1, hh):
                go(ag_copy(way, d + 1, hh))

    tile = 96 if rows % 96 == 0 else rows
    tiles = rows // tile

    def delta_tile(i, _):
        at = pl.ds(pl.multiple_of(i * tile, tile), tile)
        a, b, dh = pre_a[at].astype(F32), pre_b[at].astype(F32), hid[at].astype(F32)
        s = 1.0 / (1.0 + jnp.exp(-a))
        delta[at, 0:ff] = (dh * b * s * (1.0 + a * (1.0 - s))).astype(BF)
        delta[at, ff:2 * ff] = (dh * a * s).astype(BF)
        return 0

    def perm_block(i, _):
        c, r = i // PLANE, i % PLANE
        other = flip(xl, r // 2) * 2 + flip(co, r % 2)
        rr = lax.broadcasted_iota(I32, (ch, 1), 0)
        m = jnp.zeros((ch, 1), I32)
        for k in range(1, n2):
            m += jnp.where(rr >= k * cap, 1, 0)
        p = m + c * n2
        low = p & 1
        off = jnp.where(low == 0, p >> 1, -((p + 1) >> 1))
        zz = off + z
        zz = jnp.where(zz < 0, zz + nz, zz)
        zz = jnp.where(zz >= nz, zz - nz, zz)
        want = zz * (PLANE * cap) + other * cap + rr - m * cap
        pick = jnp.where(lax.broadcasted_iota(I32, (ch, rows), 1) == want, 1.0, 0.0).astype(BF)
        dperm[pl.ds(pl.multiple_of(i * ch, ch), ch)] = mm(pick, delta[...]).astype(BF)
        return 0

    def turn_block(i, _):
        eye = jnp.where(
            lax.broadcasted_iota(I32, (128, 2 * ff), 0) + i * 128 == lax.broadcasted_iota(I32, (128, 2 * ff), 1), 1.0, 0.0
        ).astype(BF)
        dturn[pl.ds(pl.multiple_of(i * 128, 128), 128)] = mm_nt(eye, dperm[...]).astype(BF)
        return 0

    turns = 2 * ff // 128

    def pick_rows(p, r):
        base = ((z * PLANE + column[r]) * cap).astype(F32)
        v = meta[p, 0:topk, :] - base
        valid = (v >= 0.0) & (v < float(cap))
        row = jnp.max(jnp.where(valid, v + float((p % n2) * cap), -1.0), axis=0, keepdims=True)
        weight = jnp.sum(jnp.where(valid, meta[p, topk:2 * topk, :], 0.0), axis=0, keepdims=True)
        it = lax.broadcasted_iota(I32, (ch, tdev), 0).astype(F32)
        return jnp.where(it == row, weight, 0.0).astype(BF)

    eye_t = jnp.where(
        lax.broadcasted_iota(I32, (tdev, tdev), 0) == lax.broadcasted_iota(I32, (tdev, tdev), 1), 1.0, 0.0
    ).astype(BF)

    def combine_rows(p):
        s = jnp.concatenate([pick_rows(p, r) for r in range(PLANE)], axis=0)
        st[p] = mm_nt(eye_t, s).astype(BF)

    def select(c, r):
        s = jnp.concatenate([pick_rows(c * n2 + m, r) for m in range(n2)], axis=1)

        def body(i, _):
            at = pl.ds(pl.multiple_of(i * nt, nt), nt)
            got = mm(s, xcol[c, :, at]).astype(BF)
            if r == 0:
                xs[pl.ds(c * PLANE * ch, ch), at] = got
            else:
                xs_send[c, r - 1, :, at] = got
            return 0

        lax.fori_loop(0, width // nt, body, 0)
        if r:
            go(xd_copy(c, r))

    def slot_grads(c, r):
        lhs = dperm[pl.ds((c * PLANE + r) * ch, ch)]

        def body(i, _):
            at = pl.ds(pl.multiple_of(i * nt, nt), nt)
            got = mm_nt(lhs, wall[at]).astype(BF)
            if r == 0:
                g_all[c, 0:ch, at] = got
            else:
                g_send[c, r - 1, :, at] = got
            return 0

        lax.fori_loop(0, width // nt, body, 0)

    xcol[0, 0:tdev] = tok[...]
    split = tiles // 2
    lax.fori_loop(0, split, delta_tile, 0)
    lax.fori_loop(split, tiles, delta_tile, 0)
    ag_event()
    lax.fori_loop(PLANE, 2 * PLANE, perm_block, 0)
    ag_event()
    lax.fori_loop(0, PLANE, perm_block, 0)
    ag_event()
    wx_i = y * 2 + (1 - xh)
    send(wblock(wx_i), wblock(wx_i), wx_s, wx_r, xpeer).wait_recv()
    for dy in range(1, ny):
        go(wy_copy(dy, 1))
    lax.fori_loop(0, turns, turn_block, 0)
    near = n2 // 2

    def until(d, h):
        while queue and queue[0] <= (d, h):
            ag_event()

    until(n2 // 2, 1)
    for r in (2, 3):
        select(0, r)
    ag_event()
    for dy in range(1, ny):
        for rel in range(2):
            wy_wait(dy, rel)
    for r in (2, 3):
        slot_grads(1, r)
        go(gd_copy(1, r))
    ag_event()
    for r in (1, 0):
        slot_grads(1, r)
        if r:
            go(gd_copy(1, r))
    for r in (1, 0):
        select(0, r)
    ag_event()
    for r in (2, 3):
        slot_grads(0, r)
    ag_event()
    for r in (1, 0):
        slot_grads(0, r)
    for p in range(n2):
        combine_rows(p)
    ag_event()
    until(n2, 0)
    for r in (2, 3, 1, 0):
        select(1, r)
    for r in (2, 3, 1):
        go(gd_copy(0, r))
    for p in range(n2, nz):
        combine_rows(p)

    def rs_event(way, d, h):
        buf = fwd if way == 0 else bwd
        p = pos(d if way == 0 else -d)
        c = p // n2
        first = d == n2 or (d == n2 - 1 and h != way)
        lhs = st[p, h * half:(h + 1) * half]

        def body(i, _):
            at = pl.ds(pl.multiple_of(i * nt, nt), nt)
            tsum[way, :, at] = mm(lhs, g_all[c, :, at])
            return 0

        lax.fori_loop(0, width // nt, body, 0)
        if first:
            buf[d, h] = tsum[way].astype(BF)
        else:
            rs_copy(way, d + 1, h).wait_recv()
            buf[d, h] = (tsum[way] + buf[d, h].astype(F32)).astype(BF)
        go(rs_copy(way, d, h))

    def part_block(dy, rel):
        i = lax.rem(y + dy, ny) * 2 + flip(xh, rel)
        at = pl.ds(pl.multiple_of(i * db, db), db)
        part[dy, rel] = mm(dturn[...], xs[:, at]).astype(BF)
        if dy:
            go(py_copy(dy, rel))

    order = [(dy, rel) for dy in (2, 1, 3) if dy < ny for rel in (1, 0)] + [(0, 1), (0, 0)]
    g_waited = set()

    def need(c):
        if c not in g_waited:
            g_waited.add(c)
            for r in range(1, PLANE):
                gd_copy(c, r).wait_recv()

    steps = [(way, d, h) for d in range(n2, 0, -1) for h in range(2) for way in range(2) if d < n2 or h == way]
    waited_x = False
    for k, (way, d, h) in enumerate(steps):
        need(pos(d if way == 0 else -d) // n2)
        rs_event(way, d, h)
        if k >= min(6, len(steps) - 2) and k % 2 == 1:
            if not waited_x:
                waited_x = True
                for c in range(2):
                    for r in range(1, PLANE):
                        xd_copy(c, r).wait_recv()
            for _ in range(2):
                if order:
                    part_block(*order.pop(0))
    while order:
        part_block(*order.pop(0))

    def ysum(rel):
        total = part[0, rel].astype(F32)
        for dy in range(1, ny):
            total += prow[dy - 1, rel].astype(F32)
        return total

    for dy in range(1, ny):
        py_copy(dy, 1).wait_recv()
    xsend[...] = ysum(1).astype(BF)
    go(px)
    for h in range(2):
        lhs = st[0, h * half:(h + 1) * half]
        for n in range(width // nt):
            at = slice(n * nt, (n + 1) * nt)
            tsum[h, :, at] = mm(lhs, g_all[0, :, at])
    for dy in range(1, ny):
        py_copy(dy, 0).wait_recv()
    px.wait_recv()
    total = (ysum(0) + xrow[...].astype(F32)).astype(BF)
    eye_d = jnp.where(
        lax.broadcasted_iota(I32, (db, db), 0) == lax.broadcasted_iota(I32, (db, db), 1), 1.0, 0.0
    ).astype(BF)
    turned = mm_nt(eye_d, total).astype(BF)
    gate_out[...] = turned[:, 0:ff]
    up_out[...] = turned[:, ff:2 * ff]
    for h in range(2):
        for way in range(2):
            rs_copy(way, 1, h).wait_recv()
        tok_out[h * half:(h + 1) * half] = (tsum[h] + fwd[0, h].astype(F32) + bwd[0, h].astype(F32)).astype(BF)
    for copy in started:
        copy.wait_send()


def on_device(nz, ny, tokens, expert_ids, keep_mask, gate_weights, hidden_grad, gate_pre, up_pre, gate_proj, up_proj):
    tdev, width = tokens.shape
    topk = expert_ids.shape[1]
    rows, ff = hidden_grad.shape[2:]
    cap = rows // (nz * PLANE)
    n2 = nz // 2
    ch = n2 * cap
    db = gate_proj.shape[1]
    dma = pltpu.SemaphoreType.DMA
    vm = pl.BlockSpec(memory_space=pltpu.VMEM)
    grads = jax.ShapeDtypeStruct((db, ff), BF)
    out = pl.pallas_call(
        functools.partial(kernel, nz, ny, cap, topk),
        out_shape=(jax.ShapeDtypeStruct((tdev, width), BF), grads, grads),
        in_specs=[vm] * 9,
        out_specs=(vm, vm, vm),
        scratch_shapes=[
            pltpu.VMEM((2, n2 * tdev, width), BF),
            pltpu.VMEM((nz, 2 * topk, tdev), F32),
            pltpu.VMEM((rows, 2 * ff), BF),
            pltpu.VMEM((rows, 2 * ff), BF),
            pltpu.VMEM((2 * ff, rows), BF),
            pltpu.VMEM((width, 2 * ff), BF),
            pltpu.VMEM((nz, tdev, PLANE * ch), BF),
            pltpu.VMEM((2, PLANE - 1, ch, width), BF),
            pltpu.VMEM((rows, width), BF),
            pltpu.VMEM((2, PLANE - 1, ch, width), BF),
            pltpu.VMEM((2, PLANE * ch, width), BF),
            pltpu.VMEM((n2 + 1, 2, tdev // 2, width), BF),
            pltpu.VMEM((n2 + 1, 2, tdev // 2, width), BF),
            pltpu.VMEM((2, tdev // 2, width), F32),
            pltpu.VMEM((ny, 2, 2 * ff, db), BF),
            pltpu.VMEM((max(ny - 1, 1), 2, 2 * ff, db), BF),
            pltpu.VMEM((2 * ff, db), BF),
            pltpu.VMEM((2 * ff, db), BF),
            dma((2, 2 * n2 + 2)), dma((2, 2 * n2 + 2)),
            dma((2, n2 + 1)), dma((2, n2 + 1)),
            dma((2, PLANE)), dma((2, PLANE)),
            dma((2, PLANE)), dma((2, PLANE)),
            dma, dma,
            dma((ny, 2)), dma((ny, 2)),
            dma((2, 2 * n2 + 2)), dma((2, 2 * n2 + 2)),
            dma((ny, 2)), dma((ny, 2)),
            dma, dma,
        ],
        compiler_params=pltpu.CompilerParams(
            collective_id=0, has_side_effects=True, vmem_limit_bytes=61000 * 1024
        ),
        cost_estimate=pl.CostEstimate(
            flops=2 * rows * width * ff * 4, bytes_accessed=6 * rows * ff + 4 * tdev * width, transcendentals=rows * ff
        ),
    )(
        expert_ids.T, keep_mask.T, gate_weights.T.astype(F32), tokens,
        hidden_grad[0, 0], gate_pre[0, 0], up_pre[0, 0], gate_proj[0], up_proj[0],
    )
    return out[0], out[1][None], out[2][None]


def solution(mesh):
    nz, ny = mesh.shape["expert"] // PLANE, mesh.shape["dp"] // 2
    both = P(("dp", "expert"), None)
    acts = P("dp", "expert", None, None)
    weights = P("expert", "dp", None)
    return jax.shard_map(
        functools.partial(on_device, nz, ny),
        mesh=mesh,
        in_specs=(both, both, both, both, acts, acts, acts, weights, weights),
        out_specs=(both, weights, weights),
        check_vma=False,
    )
```

```python
import functools

import jax
import jax.numpy as jnp
from jax import lax
from jax.experimental import pallas as pl
from jax.experimental.pallas import tpu as pltpu
from jax.sharding import PartitionSpec as P

MESH = pl.DeviceIdType.MESH
BF = jnp.bfloat16
F32 = jnp.float32
I32 = jnp.int32
NPA = 2
NPR = 2
PLANE = 4


def mm_nt(a, b):
    return lax.dot_general(a, b, (((1,), (1,)), ((), ())), preferred_element_type=F32)


def mm(a, b):
    return jnp.dot(a, b, preferred_element_type=F32)


def flip(bit, by):
    return bit + by - 2 * bit * by


def kernel(
    nz, ny, cap, topk,
    ids_in, keep_in, gate_in, tok, hid, pre_a, pre_b, w_gate, w_up,
    tok_out, gate_out, up_out,
    xcol, meta, delta, dperm, dturn, wall, st, xs_send, xs, g_send, g_all,
    fwd, bwd, tsum, part, prow, xsend, xrow,
    ag_s, ag_r, me_s, me_r, xd_s, xd_r, gd_s, gd_r, wx_s, wx_r, wy_s, wy_r,
    rs_s, rs_r, py_s, py_r, px_s, px_r,
):
    n2 = nz // 2
    tdev, width = tok.shape
    cut, rcut = tdev // NPA, tdev // NPR
    ff = w_gate.shape[1]
    rows = hid.shape[0]
    ch = n2 * cap
    low = (n2 // 2) * cap // 16 * 16
    span = ((0, low), (low, ch - low))
    held = (range(0, -(-low // cap)), range(low // cap, n2))
    db = w_gate.shape[0]
    nt = min(512, width)
    e_ix, d_ix = lax.axis_index("expert"), lax.axis_index("dp")
    z, q = e_ix // PLANE, e_ix % PLANE
    xl, co = q // 2, q % 2
    y, xh = d_ix // 2, d_ix % 2
    zup = (d_ix, lax.rem(z + 1, nz) * PLANE + q)
    zdn = (d_ix, lax.rem(z + nz - 1, nz) * PLANE + q)
    column = [flip(xl, r // 2) * 2 + flip(co, r % 2) for r in range(PLANE)]
    plane = [(d_ix, z * PLANE + column[r]) for r in range(PLANE)]
    ypeer = [(lax.rem(y + dy, ny) * 2 + xh, e_ix) for dy in range(ny)]
    xpeer = (y * 2 + (1 - xh), e_ix)

    def pos(off):
        if off == -n2 or off == n2:
            return nz - 1
        return 2 * off if off >= 0 else -2 * off - 1

    def send(src, dst, s, r, dev):
        return pltpu.make_async_remote_copy(
            src_ref=src, dst_ref=dst, send_sem=s, recv_sem=r, device_id=dev, device_id_type=MESH
        )

    def slot_piece(p, h):
        return xcol.at[p // n2, pl.ds((p % n2) * tdev + h * cut, cut)]

    def ag_copy(way, d, h):
        sign = -1 if way == 0 else 1
        src = tok.at[pl.ds(h * cut, cut)] if d == 1 else slot_piece(pos(sign * (d - 1)), h)
        ix = (way, d * NPA + h)
        return send(src, slot_piece(pos(sign * d), h), ag_s.at[ix], ag_r.at[ix], zup if way == 0 else zdn)

    def me_copy(way, d):
        sign = -1 if way == 0 else 1
        ix = (way, d)
        return send(meta.at[pos(sign * (d - 1))], meta.at[pos(sign * d)], me_s.at[ix], me_r.at[ix], zup if way == 0 else zdn)

    def xd_copy(c, r, w):
        at, n = span[w]
        ix = (c * 2 + w, r)
        return send(xs_send.at[c, r - 1, pl.ds(at, n)], xs.at[pl.ds((c * PLANE + r) * ch + at, n)], xd_s.at[ix], xd_r.at[ix], plane[r])

    def g_rows(c, w):
        return (c * ch + span[w][0]) * PLANE

    def gd_copy(c, r, w):
        at, n = span[w]
        ix = (c * 2 + w, r)
        return send(g_send.at[c, r - 1, pl.ds(at, n)], g_all.at[pl.ds(g_rows(c, w) + r * n, n)], gd_s.at[ix], gd_r.at[ix], plane[r])

    def wblock(i):
        return wall.at[pl.ds(pl.multiple_of(i * db, db), db)]

    wx = send(wblock(d_ix), wblock(d_ix), wx_s, wx_r, xpeer)

    def wy_copy(dy, rel):
        i = y * 2 + flip(xh, rel)
        return send(wblock(i), wblock(i), wy_s.at[dy, rel], wy_r.at[dy, rel], ypeer[dy])

    def wy_wait(dy, rel):
        i = lax.rem(y + ny - dy, ny) * 2 + flip(xh, rel)
        send(wblock(i), wblock(i), wy_s.at[dy, rel], wy_r.at[dy, rel], ypeer[dy]).wait_recv()

    def rs_copy(way, d, h):
        buf = fwd if way == 0 else bwd
        ix = (way, d * NPR + h)
        return send(buf.at[d, h], buf.at[d - 1, h], rs_s.at[ix], rs_r.at[ix], zup if way == 0 else zdn)

    def py_copy(dy, rel):
        return send(part.at[dy, rel], prow.at[dy - 1, rel], py_s.at[dy, rel], py_r.at[dy, rel], ypeer[dy])

    px = send(xsend, xrow, px_s, px_r, xpeer)
    started = []

    def go(copy):
        copy.start()
        started.append(copy)

    barrier = pltpu.get_barrier_semaphore()
    partners = [zup, zdn, xpeer] + plane[1:] + ypeer[1:]
    for dev in partners:
        pl.semaphore_signal(barrier, inc=1, device_id=dev, device_id_type=MESH)

    experts = nz * PLANE
    ids, keep = ids_in[...], keep_in[...]
    e_iota = lax.broadcasted_iota(I32, (experts, tdev), 0)
    named = jnp.zeros((experts, tdev), F32)
    for k in range(topk):
        named += jnp.where((e_iota == ids[k:k + 1, :]) & (keep[k:k + 1, :] > 0), 1.0, 0.0)
    earlier = jnp.where(
        lax.broadcasted_iota(I32, (tdev, tdev), 0) < lax.broadcasted_iota(I32, (tdev, tdev), 1), 1.0, 0.0
    ).astype(BF)
    before = mm(named.astype(BF), earlier)
    for k in range(topk):
        mine = ids[k:k + 1, :]
        slot = jnp.sum(jnp.where(e_iota == mine, before, 0.0), axis=0, keepdims=True)
        row = mine.astype(F32) * float(cap) + slot
        meta[0, k:k + 1, :] = jnp.where(keep[k:k + 1, :] > 0, row, -4096.0)
    meta[0, topk:2 * topk, :] = gate_in[...]
    mine_w = pl.ds(pl.multiple_of(d_ix * db, db), db)
    wall[mine_w, 0:ff] = w_gate[...]
    wall[mine_w, ff:2 * ff] = w_up[...]

    pl.semaphore_wait(barrier, len(partners))

    def ag_has(way, d, h):
        return d < n2 or (d == n2 and h // (NPA // 2) == way)

    def me_has(way, d):
        return d < n2 or (d == n2 and way == 0)

    for way in range(2):
        go(me_copy(way, 1))
    for h in range(NPA):
        for way in range(2):
            if ag_has(way, 1, h):
                go(ag_copy(way, 1, h))
    go(wx)
    for dy in range(1, ny):
        go(wy_copy(dy, 0))

    events = [(d, h) for d in range(1, n2) for h in range(NPA)] + [(n2, h) for h in range(NPA // 2)]
    queue = list(events)

    def ag_event():
        if not queue:
            return
        d, h = queue.pop(0)
        for way in range(2):
            if h == 0 and me_has(way, d) and d < n2:
                me_copy(way, d).wait_recv()
                if me_has(way, d + 1):
                    go(me_copy(way, d + 1))
        for way in range(2):
            hh = h + way * (NPA // 2) if d == n2 else h
            ag_copy(way, d, hh).wait_recv()
            if ag_has(way, d + 1, hh):
                go(ag_copy(way, d + 1, hh))

    tile = 96 if rows % 96 == 0 else rows
    tiles = rows // tile

    def delta_tile(i, _):
        at = pl.ds(pl.multiple_of(i * tile, tile), tile)
        a, b, dh = pre_a[at].astype(F32), pre_b[at].astype(F32), hid[at].astype(F32)
        s = 1.0 / (1.0 + jnp.exp(-a))
        delta[at, 0:ff] = (dh * b * s * (1.0 + a * (1.0 - s))).astype(BF)
        delta[at, ff:2 * ff] = (dh * a * s).astype(BF)
        return 0

    def perm_block(i, _):
        c, r = i // PLANE, i % PLANE
        other = flip(xl, r // 2) * 2 + flip(co, r % 2)
        rr = lax.broadcasted_iota(I32, (ch, 1), 0)
        m = jnp.zeros((ch, 1), I32)
        for k in range(1, n2):
            m += jnp.where(rr >= k * cap, 1, 0)
        p = m + c * n2
        low = p & 1
        off = jnp.where(low == 0, p >> 1, -((p + 1) >> 1))
        zz = off + z
        zz = jnp.where(zz < 0, zz + nz, zz)
        zz = jnp.where(zz >= nz, zz - nz, zz)
        want = zz * (PLANE * cap) + other * cap + rr - m * cap
        pick = jnp.where(lax.broadcasted_iota(I32, (ch, rows), 1) == want, 1.0, 0.0).astype(BF)
        dperm[pl.ds(pl.multiple_of(i * ch, ch), ch)] = mm(pick, delta[...]).astype(BF)
        return 0

    def turn_block(i, _):
        eye = jnp.where(
            lax.broadcasted_iota(I32, (128, 2 * ff), 0) + i * 128 == lax.broadcasted_iota(I32, (128, 2 * ff), 1), 1.0, 0.0
        ).astype(BF)
        dturn[pl.ds(pl.multiple_of(i * 128, 128), 128)] = mm_nt(eye, dperm[...]).astype(BF)
        return 0

    turns = 2 * ff // 128

    def pick_rows(p, r, w):
        base = ((z * PLANE + column[r]) * cap).astype(F32)
        v = meta[p, 0:topk, :] - base
        valid = (v >= 0.0) & (v < float(cap))
        row = jnp.max(jnp.where(valid, v + float((p % n2) * cap - span[w][0]), -1.0), axis=0, keepdims=True)
        weight = jnp.sum(jnp.where(valid, meta[p, topk:2 * topk, :], 0.0), axis=0, keepdims=True)
        it = lax.broadcasted_iota(I32, (span[w][1], tdev), 0).astype(F32)
        return jnp.where(it == row, weight, 0.0).astype(BF)

    eye_t = jnp.where(
        lax.broadcasted_iota(I32, (tdev, tdev), 0) == lax.broadcasted_iota(I32, (tdev, tdev), 1), 1.0, 0.0
    ).astype(BF)

    def parts_of(p):
        return [w for w in range(2) if p % n2 in held[w]]

    def columns_of(w):
        return slice(span[w][0] * PLANE, (span[w][0] + span[w][1]) * PLANE)

    def combine_rows(p):
        for w in parts_of(p):
            s = jnp.concatenate([pick_rows(p, r, w) for r in range(PLANE)], axis=0)
            st[p, :, columns_of(w)] = mm_nt(eye_t, s).astype(BF)

    def combine(p, lo, n, at):
        c = p // n2
        total = None
        for w in parts_of(p):
            one = mm(st[p, lo:lo + n, columns_of(w)], g_all[pl.ds(g_rows(c, w), span[w][1] * PLANE), at])
            total = one if total is None else total + one
        return total

    def select(c, r, w):
        first, n = span[w]
        s = jnp.concatenate([pick_rows(c * n2 + m, r, w) for m in held[w]], axis=1)
        src = slice(held[w][0] * tdev, (held[w][-1] + 1) * tdev)

        def body(i, _):
            at = pl.ds(pl.multiple_of(i * nt, nt), nt)
            got = mm(s, xcol[c, src, at]).astype(BF)
            if r == 0:
                xs[pl.ds(c * PLANE * ch + first, n), at] = got
            else:
                xs_send[c, r - 1, first:first + n, at] = got
            return 0

        lax.fori_loop(0, width // nt, body, 0)
        if r:
            go(xd_copy(c, r, w))

    def slot_grads(c, r, w):
        first, n = span[w]
        lhs = dperm[pl.ds((c * PLANE + r) * ch + first, n)]

        def body(i, _):
            at = pl.ds(pl.multiple_of(i * nt, nt), nt)
            got = mm_nt(lhs, wall[at]).astype(BF)
            if r == 0:
                g_all[pl.ds(g_rows(c, w), n), at] = got
            else:
                g_send[c, r - 1, first:first + n, at] = got
            return 0

        lax.fori_loop(0, width // nt, body, 0)

    def until(d, h):
        while queue and queue[0] <= (d, h):
            ag_event()

    away = (2, 3, 1)

    xcol[0, 0:tdev] = tok[...]
    lax.fori_loop(0, tiles, delta_tile, 0)
    ag_event()
    lax.fori_loop(PLANE, 2 * PLANE, perm_block, 0)
    ag_event()
    wx_i = y * 2 + (1 - xh)
    send(wblock(wx_i), wblock(wx_i), wx_s, wx_r, xpeer).wait_recv()
    for dy in range(1, ny):
        go(wy_copy(dy, 1))
    lax.fori_loop(0, PLANE, perm_block, 0)
    ag_event()
    lax.fori_loop(0, turns, turn_block, 0)
    until((held[0][-1] + 1) // 2, NPA)
    for r in away + (0,):
        select(0, r, 0)
    ag_event()
    for p in range(n2 // 2):
        combine_rows(p)
    ag_event()
    for dy in range(1, ny):
        for rel in range(2):
            wy_wait(dy, rel)
    for r in away:
        slot_grads(1, r, 1)
        go(gd_copy(1, r, 1))
    ag_event()
    slot_grads(1, 0, 1)
    until(n2 // 2, NPA)
    for r in away:
        select(0, r, 1)
    for r in away:
        slot_grads(1, r, 0)
        go(gd_copy(1, r, 0))
    ag_event()
    select(0, 0, 1)
    slot_grads(1, 0, 0)
    for p in range(n2 // 2, n2):
        combine_rows(p)
    ag_event()
    for r in range(PLANE):
        slot_grads(0, r, 1)
    ag_event()
    until((n2 + held[0][-1] + 1) // 2, NPA)
    for r in away + (0,):
        select(1, r, 0)
    ag_event()
    for r in away:
        go(gd_copy(0, r, 1))
    for r in range(PLANE):
        slot_grads(0, r, 0)
    until(n2 - 1, NPA - 1)
    me_copy(0, n2).wait_recv()
    for p in range(n2, nz):
        combine_rows(p)

    def rs_event(way, d, h):
        buf = fwd if way == 0 else bwd
        p = pos(d if way == 0 else -d)
        first = d == n2 or (d == n2 - 1 and h // (NPR // 2) != way)

        def body(i, _):
            at = pl.ds(pl.multiple_of(i * nt, nt), nt)
            tsum[way, :, at] = combine(p, h * rcut, rcut, at)
            return 0

        lax.fori_loop(0, width // nt, body, 0)
        if first:
            buf[d, h] = tsum[way].astype(BF)
        else:
            rs_copy(way, d + 1, h).wait_recv()
            buf[d, h] = (tsum[way] + buf[d, h].astype(F32)).astype(BF)
        go(rs_copy(way, d, h))

    def part_block(dy, rel):
        i = lax.rem(y + dy, ny) * 2 + flip(xh, rel)
        at = pl.ds(pl.multiple_of(i * db, db), db)
        part[dy, rel] = mm(dturn[...], xs[:, at]).astype(BF)
        if dy:
            go(py_copy(dy, rel))

    g_waited = set()

    def need(p):
        for w in parts_of(p):
            if (p // n2, w) not in g_waited:
                g_waited.add((p // n2, w))
                for r in range(1, PLANE):
                    gd_copy(p // n2, r, w).wait_recv()

    far = [dy for dy in (2, 1, 3) if dy < ny]

    def xd_wait():
        for c in range(2):
            for w in range(2):
                for r in range(1, PLANE):
                    xd_copy(c, r, w).wait_recv()

    def parts_away(rel):
        for dy in far:
            part_block(dy, rel)

    def parts_own():
        for rel in (1, 0):
            part_block(0, rel)

    def ysum(rel):
        total = part[0, rel].astype(F32)
        for dy in range(1, ny):
            total += prow[dy - 1, rel].astype(F32)
        return total

    def cross():
        for dy in range(1, ny):
            py_copy(dy, 1).wait_recv()
        xsend[...] = ysum(1).astype(BF)
        go(px)

    def last_rows():
        until(n2, NPA)
        for r in away + (0,):
            select(1, r, 1)
        for r in away:
            go(gd_copy(0, r, 0))

    steps = [(way, d, h) for d in range(n2, 0, -1) for h in range(NPR) for way in range(2) if d < n2 or h // (NPR // 2) == way]
    pairs = len(steps) // 2
    todo = [(1, last_rows), (pairs - 7, xd_wait), (pairs - 7, functools.partial(parts_away, 1)),
            (pairs - 6, functools.partial(parts_away, 0)), (pairs - 5, parts_own), (pairs - 2, cross)]
    for j in range(pairs):
        for way, d, h in steps[2 * j:2 * j + 2]:
            need(pos(d if way == 0 else -d))
            rs_event(way, d, h)
        while todo and todo[0][0] <= j:
            todo.pop(0)[1]()
    for _, what in todo:
        what()

    need(0)
    for h in range(NPR):
        for n in range(width // nt):
            at = slice(n * nt, (n + 1) * nt)
            tsum[h, :, at] = combine(0, h * rcut, rcut, at)
    for dy in range(1, ny):
        py_copy(dy, 0).wait_recv()
    px.wait_recv()
    total = (ysum(0) + xrow[...].astype(F32)).astype(BF)
    eye_d = jnp.where(
        lax.broadcasted_iota(I32, (db, db), 0) == lax.broadcasted_iota(I32, (db, db), 1), 1.0, 0.0
    ).astype(BF)
    turned = mm_nt(eye_d, total).astype(BF)
    gate_out[...] = turned[:, 0:ff]
    up_out[...] = turned[:, ff:2 * ff]
    for h in range(NPR):
        for way in range(2):
            rs_copy(way, 1, h).wait_recv()
        tok_out[h * rcut:(h + 1) * rcut] = (tsum[h] + fwd[0, h].astype(F32) + bwd[0, h].astype(F32)).astype(BF)
    for copy in started:
        copy.wait_send()


def on_device(nz, ny, tokens, expert_ids, keep_mask, gate_weights, hidden_grad, gate_pre, up_pre, gate_proj, up_proj):
    tdev, width = tokens.shape
    topk = expert_ids.shape[1]
    rows, ff = hidden_grad.shape[2:]
    cap = rows // (nz * PLANE)
    n2 = nz // 2
    ch = n2 * cap
    db = gate_proj.shape[1]
    dma = pltpu.SemaphoreType.DMA
    vm = pl.BlockSpec(memory_space=pltpu.VMEM)
    grads = jax.ShapeDtypeStruct((db, ff), BF)
    out = pl.pallas_call(
        functools.partial(kernel, nz, ny, cap, topk),
        out_shape=(jax.ShapeDtypeStruct((tdev, width), BF), grads, grads),
        in_specs=[vm] * 9,
        out_specs=(vm, vm, vm),
        scratch_shapes=[
            pltpu.VMEM((2, n2 * tdev, width), BF),
            pltpu.VMEM((nz, 2 * topk, tdev), F32),
            pltpu.VMEM((rows, 2 * ff), BF),
            pltpu.VMEM((rows, 2 * ff), BF),
            pltpu.VMEM((2 * ff, rows), BF),
            pltpu.VMEM((width, 2 * ff), BF),
            pltpu.VMEM((nz, tdev, PLANE * ch), BF),
            pltpu.VMEM((2, PLANE - 1, ch, width), BF),
            pltpu.VMEM((rows, width), BF),
            pltpu.VMEM((2, PLANE - 1, ch, width), BF),
            pltpu.VMEM((rows, width), BF),
            pltpu.VMEM((n2 + 1, NPR, tdev // NPR, width), BF),
            pltpu.VMEM((n2 + 1, NPR, tdev // NPR, width), BF),
            pltpu.VMEM((NPR, tdev // NPR, width), F32),
            pltpu.VMEM((ny, 2, 2 * ff, db), BF),
            pltpu.VMEM((max(ny - 1, 1), 2, 2 * ff, db), BF),
            pltpu.VMEM((2 * ff, db), BF),
            pltpu.VMEM((2 * ff, db), BF),
            dma((2, NPA * (n2 + 1))), dma((2, NPA * (n2 + 1))),
            dma((2, n2 + 1)), dma((2, n2 + 1)),
            dma((4, PLANE)), dma((4, PLANE)),
            dma((4, PLANE)), dma((4, PLANE)),
            dma, dma,
            dma((ny, 2)), dma((ny, 2)),
            dma((2, NPR * (n2 + 1))), dma((2, NPR * (n2 + 1))),
            dma((ny, 2)), dma((ny, 2)),
            dma, dma,
        ],
        compiler_params=pltpu.CompilerParams(
            collective_id=0, has_side_effects=True, vmem_limit_bytes=61000 * 1024
        ),
        cost_estimate=pl.CostEstimate(
            flops=2 * rows * width * ff * 4, bytes_accessed=6 * rows * ff + 4 * tdev * width, transcendentals=rows * ff
        ),
    )(
        expert_ids.T, keep_mask.T, gate_weights.T.astype(F32), tokens,
        hidden_grad[0, 0], gate_pre[0, 0], up_pre[0, 0], gate_proj[0], up_proj[0],
    )
    return out[0], out[1][None], out[2][None]


def solution(mesh):
    nz, ny = mesh.shape["expert"] // PLANE, mesh.shape["dp"] // 2
    both = P(("dp", "expert"), None)
    acts = P("dp", "expert", None, None)
    weights = P("expert", "dp", None)
    return jax.shard_map(
        functools.partial(on_device, nz, ny),
        mesh=mesh,
        in_specs=(both, both, both, both, acts, acts, acts, weights, weights),
        out_specs=(both, weights, weights),
        check_vma=False,
    )
```

```python
import functools

import jax
import jax.numpy as jnp
from jax import lax
from jax.experimental import pallas as pl
from jax.experimental.pallas import tpu as pltpu
from jax.sharding import PartitionSpec as P

MESH = pl.DeviceIdType.MESH
BF = jnp.bfloat16
F32 = jnp.float32
I32 = jnp.int32
NPA = 2
NPR = 2
PLANE = 4


def mm_nt(a, b):
    return lax.dot_general(a, b, (((1,), (1,)), ((), ())), preferred_element_type=F32)


def mm(a, b):
    return jnp.dot(a, b, preferred_element_type=F32)


def flip(bit, by):
    return bit + by - 2 * bit * by


def kernel(
    nz, ny, cap, topk,
    ids_in, keep_in, gate_in, tok, hid_in, pre_a_in, pre_b_in, w_gate, w_up,
    tok_out, gate_out, up_out,
    xcol, meta, delta, dperm, dturn, wall, st, xs_send, xs, g_send, g_all,
    fwd, bwd, tsum, part, prow, xsend, xrow,
    ag_s, ag_r, me_s, me_r, xd_s, xd_r, gd_s, gd_r, wx_s, wx_r, wy_s, wy_r,
    rs_s, rs_r, py_s, py_r, px_s, px_r, hid, pre_a, pre_b, in_s,
):
    n2 = nz // 2
    tdev, width = tok.shape
    cut, rcut = tdev // NPA, tdev // NPR
    ff = w_gate.shape[1]
    rows = hid.shape[0]
    ch = n2 * cap
    low = (n2 // 2) * cap // 16 * 16
    span = ((0, low), (low, ch - low))
    held = (range(0, -(-low // cap)), range(low // cap, n2))
    db = w_gate.shape[0]
    nt = min(512, width)
    e_ix, d_ix = lax.axis_index("expert"), lax.axis_index("dp")
    z, q = e_ix // PLANE, e_ix % PLANE
    xl, co = q // 2, q % 2
    y, xh = d_ix // 2, d_ix % 2
    zup = (d_ix, lax.rem(z + 1, nz) * PLANE + q)
    zdn = (d_ix, lax.rem(z + nz - 1, nz) * PLANE + q)
    column = [flip(xl, r // 2) * 2 + flip(co, r % 2) for r in range(PLANE)]
    plane = [(d_ix, z * PLANE + column[r]) for r in range(PLANE)]
    ypeer = [(lax.rem(y + dy, ny) * 2 + xh, e_ix) for dy in range(ny)]
    xpeer = (y * 2 + (1 - xh), e_ix)

    def pos(off):
        if off == -n2 or off == n2:
            return nz - 1
        return 2 * off if off >= 0 else -2 * off - 1

    def send(src, dst, s, r, dev):
        return pltpu.make_async_remote_copy(
            src_ref=src, dst_ref=dst, send_sem=s, recv_sem=r, device_id=dev, device_id_type=MESH
        )

    def slot_piece(p, h):
        return xcol.at[p // n2, pl.ds((p % n2) * tdev + h * cut, cut)]

    def ag_copy(way, d, h):
        sign = -1 if way == 0 else 1
        src = slot_piece(pos(sign * (d - 1)), h)
        ix = (way, d * NPA + h)
        return send(src, slot_piece(pos(sign * d), h), ag_s.at[ix], ag_r.at[ix], zup if way == 0 else zdn)

    def me_copy(way, d):
        sign = -1 if way == 0 else 1
        ix = (way, d)
        return send(meta.at[pos(sign * (d - 1))], meta.at[pos(sign * d)], me_s.at[ix], me_r.at[ix], zup if way == 0 else zdn)

    def xd_copy(c, r, w):
        at, n = span[w]
        ix = (c * 2 + w, r)
        return send(xs_send.at[c, r - 1, pl.ds(at, n)], xs.at[pl.ds((c * PLANE + r) * ch + at, n)], xd_s.at[ix], xd_r.at[ix], plane[r])

    def g_rows(c, w):
        return (c * ch + span[w][0]) * PLANE

    def gd_copy(c, r, w):
        at, n = span[w]
        ix = (c * 2 + w, r)
        return send(g_send.at[c, r - 1, pl.ds(at, n)], g_all.at[pl.ds(g_rows(c, w) + r * n, n)], gd_s.at[ix], gd_r.at[ix], plane[r])

    def wblock(i):
        return wall.at[pl.ds(pl.multiple_of(i * db, db), db)]

    wx = send(wblock(d_ix), wblock(d_ix), wx_s, wx_r, xpeer)

    def wy_copy(dy, rel):
        i = y * 2 + flip(xh, rel)
        return send(wblock(i), wblock(i), wy_s.at[dy, rel], wy_r.at[dy, rel], ypeer[dy])

    def wy_wait(dy, rel):
        i = lax.rem(y + ny - dy, ny) * 2 + flip(xh, rel)
        send(wblock(i), wblock(i), wy_s.at[dy, rel], wy_r.at[dy, rel], ypeer[dy]).wait_recv()

    def rs_copy(way, d, h):
        buf = fwd if way == 0 else bwd
        ix = (way, d * NPR + h)
        return send(buf.at[d, h], buf.at[d - 1, h], rs_s.at[ix], rs_r.at[ix], zup if way == 0 else zdn)

    def py_copy(dy, rel):
        return send(part.at[dy, rel], prow.at[dy - 1, rel], py_s.at[dy, rel], py_r.at[dy, rel], ypeer[dy])

    px = send(xsend, xrow, px_s, px_r, xpeer)
    started = []

    def go(copy):
        copy.start()
        started.append(copy)

    barrier = pltpu.get_barrier_semaphore()
    partners = [zup, zdn, xpeer] + plane[1:] + ypeer[1:]
    for dev in partners:
        pl.semaphore_signal(barrier, inc=1, device_id=dev, device_id_type=MESH)

    mine_w = pl.ds(pl.multiple_of(d_ix * db, db), db)
    fetch_w = [
        pltpu.make_async_copy(w_gate, wall.at[mine_w, pl.ds(0, ff)], in_s.at[0]),
        pltpu.make_async_copy(w_up, wall.at[mine_w, pl.ds(ff, ff)], in_s.at[1]),
    ]
    fetch = [
        pltpu.make_async_copy(hid_in, hid, in_s.at[2]),
        pltpu.make_async_copy(pre_a_in, pre_a, in_s.at[3]),
        pltpu.make_async_copy(pre_b_in, pre_b, in_s.at[4]),
        pltpu.make_async_copy(tok, xcol.at[0, pl.ds(0, tdev)], in_s.at[5]),
    ]
    for copy in fetch[3:] + fetch_w + fetch[:3]:
        copy.start()

    experts = nz * PLANE
    ids, keep = ids_in[...], keep_in[...]
    e_iota = lax.broadcasted_iota(I32, (experts, tdev), 0)
    named = jnp.zeros((experts, tdev), F32)
    for k in range(topk):
        named += jnp.where((e_iota == ids[k:k + 1, :]) & (keep[k:k + 1, :] > 0), 1.0, 0.0)
    earlier = jnp.where(
        lax.broadcasted_iota(I32, (tdev, tdev), 0) < lax.broadcasted_iota(I32, (tdev, tdev), 1), 1.0, 0.0
    ).astype(BF)
    before = mm(named.astype(BF), earlier)
    for k in range(topk):
        mine = ids[k:k + 1, :]
        slot = jnp.sum(jnp.where(e_iota == mine, before, 0.0), axis=0, keepdims=True)
        row = mine.astype(F32) * float(cap) + slot
        meta[0, k:k + 1, :] = jnp.where(keep[k:k + 1, :] > 0, row, -4096.0)
    meta[0, topk:2 * topk, :] = gate_in[...].astype(F32)

    pl.semaphore_wait(barrier, len(partners))

    def ag_has(way, d, h):
        return d < n2 or (d == n2 and h // (NPA // 2) == way)

    def me_has(way, d):
        return d < n2 or (d == n2 and way == 0)

    fetch[3].wait()
    for way in range(2):
        go(me_copy(way, 1))
    for h in range(NPA):
        for way in range(2):
            if ag_has(way, 1, h):
                go(ag_copy(way, 1, h))
    for copy in fetch_w:
        copy.wait()
    go(wx)
    for dy in range(1, ny):
        go(wy_copy(dy, 0))

    events = [(d, h) for d in range(1, n2) for h in range(NPA)] + [(n2, h) for h in range(NPA // 2)]
    queue = list(events)

    def ag_event():
        if not queue:
            return
        d, h = queue.pop(0)
        for way in range(2):
            if h == 0 and me_has(way, d) and d < n2:
                me_copy(way, d).wait_recv()
                if me_has(way, d + 1):
                    go(me_copy(way, d + 1))
        for way in range(2):
            hh = h + way * (NPA // 2) if d == n2 else h
            ag_copy(way, d, hh).wait_recv()
            if ag_has(way, d + 1, hh):
                go(ag_copy(way, d + 1, hh))

    tile = 96 if rows % 96 == 0 else rows
    tiles = rows // tile

    def delta_tile(i, _):
        at = pl.ds(pl.multiple_of(i * tile, tile), tile)
        a, b, dh = pre_a[at].astype(F32), pre_b[at].astype(F32), hid[at].astype(F32)
        s = 1.0 / (1.0 + jnp.exp(-a))
        delta[at, 0:ff] = (dh * b * s * (1.0 + a * (1.0 - s))).astype(BF)
        delta[at, ff:2 * ff] = (dh * a * s).astype(BF)
        return 0

    def perm_block(i, _):
        c, r = i // PLANE, i % PLANE
        other = flip(xl, r // 2) * 2 + flip(co, r % 2)
        rr = lax.broadcasted_iota(I32, (ch, 1), 0)
        m = jnp.zeros((ch, 1), I32)
        for k in range(1, n2):
            m += jnp.where(rr >= k * cap, 1, 0)
        p = m + c * n2
        low = p & 1
        off = jnp.where(low == 0, p >> 1, -((p + 1) >> 1))
        zz = off + z
        zz = jnp.where(zz < 0, zz + nz, zz)
        zz = jnp.where(zz >= nz, zz - nz, zz)
        want = zz * (PLANE * cap) + other * cap + rr - m * cap
        pick = jnp.where(lax.broadcasted_iota(I32, (ch, rows), 1) == want, 1.0, 0.0).astype(BF)
        dperm[pl.ds(pl.multiple_of(i * ch, ch), ch)] = mm(pick, delta[...]).astype(BF)
        return 0

    def turn_block(i, _):
        eye = jnp.where(
            lax.broadcasted_iota(I32, (128, 2 * ff), 0) + i * 128 == lax.broadcasted_iota(I32, (128, 2 * ff), 1), 1.0, 0.0
        ).astype(BF)
        dturn[pl.ds(pl.multiple_of(i * 128, 128), 128)] = mm_nt(eye, dperm[...]).astype(BF)
        return 0

    turns = 2 * ff // 128

    def pick_rows(p, r, w):
        base = ((z * PLANE + column[r]) * cap).astype(F32)
        v = meta[p, 0:topk, :] - base
        valid = (v >= 0.0) & (v < float(cap))
        row = jnp.max(jnp.where(valid, v + float((p % n2) * cap - span[w][0]), -1.0), axis=0, keepdims=True)
        weight = jnp.sum(jnp.where(valid, meta[p, topk:2 * topk, :], 0.0), axis=0, keepdims=True)
        it = lax.broadcasted_iota(I32, (span[w][1], tdev), 0).astype(F32)
        return jnp.where(it == row, weight, 0.0).astype(BF)

    eye_t = jnp.where(
        lax.broadcasted_iota(I32, (tdev, tdev), 0) == lax.broadcasted_iota(I32, (tdev, tdev), 1), 1.0, 0.0
    ).astype(BF)

    def parts_of(p):
        return [w for w in range(2) if p % n2 in held[w]]

    def columns_of(w):
        return slice(span[w][0] * PLANE, (span[w][0] + span[w][1]) * PLANE)

    def combine_rows(p):
        for w in parts_of(p):
            s = jnp.concatenate([pick_rows(p, r, w) for r in range(PLANE)], axis=0)
            st[p, :, columns_of(w)] = mm_nt(eye_t, s).astype(BF)

    def combine(p, lo, n, at):
        c = p // n2
        total = None
        for w in parts_of(p):
            one = mm(st[p, lo:lo + n, columns_of(w)], g_all[pl.ds(g_rows(c, w), span[w][1] * PLANE), at])
            total = one if total is None else total + one
        return total

    def select(c, r, w):
        first, n = span[w]
        s = jnp.concatenate([pick_rows(c * n2 + m, r, w) for m in held[w]], axis=1)
        src = slice(held[w][0] * tdev, (held[w][-1] + 1) * tdev)

        def body(i, _):
            at = pl.ds(pl.multiple_of(i * nt, nt), nt)
            got = mm(s, xcol[c, src, at]).astype(BF)
            if r == 0:
                xs[pl.ds(c * PLANE * ch + first, n), at] = got
            else:
                xs_send[c, r - 1, first:first + n, at] = got
            return 0

        lax.fori_loop(0, width // nt, body, 0)
        if r:
            go(xd_copy(c, r, w))

    def slot_grads(c, r, w):
        first, n = span[w]
        lhs = dperm[pl.ds((c * PLANE + r) * ch + first, n)]

        def body(i, _):
            at = pl.ds(pl.multiple_of(i * nt, nt), nt)
            got = mm_nt(lhs, wall[at]).astype(BF)
            if r == 0:
                g_all[pl.ds(g_rows(c, w), n), at] = got
            else:
                g_send[c, r - 1, first:first + n, at] = got
            return 0

        lax.fori_loop(0, width // nt, body, 0)

    def until(d, h):
        while queue and queue[0] <= (d, h):
            ag_event()

    away = (2, 3, 1)

    for copy in fetch[:3]:
        copy.wait()
    lax.fori_loop(0, tiles, delta_tile, 0)
    ag_event()
    lax.fori_loop(PLANE, 2 * PLANE, perm_block, 0)
    ag_event()
    wx_i = y * 2 + (1 - xh)
    send(wblock(wx_i), wblock(wx_i), wx_s, wx_r, xpeer).wait_recv()
    for dy in range(1, ny):
        go(wy_copy(dy, 1))
    lax.fori_loop(0, PLANE, perm_block, 0)
    ag_event()
    lax.fori_loop(0, turns, turn_block, 0)
    until((held[0][-1] + 1) // 2, NPA)
    for r in away + (0,):
        select(0, r, 0)
    ag_event()
    for p in range(n2 // 2):
        combine_rows(p)
    ag_event()
    for dy in range(1, ny):
        for rel in range(2):
            wy_wait(dy, rel)
    for r in away:
        slot_grads(1, r, 1)
        go(gd_copy(1, r, 1))
    ag_event()
    slot_grads(1, 0, 1)
    until(n2 // 2, NPA)
    for r in away:
        select(0, r, 1)
    for r in away:
        slot_grads(1, r, 0)
        go(gd_copy(1, r, 0))
    ag_event()
    select(0, 0, 1)
    slot_grads(1, 0, 0)
    for p in range(n2 // 2, n2):
        combine_rows(p)
    ag_event()
    for r in range(PLANE):
        slot_grads(0, r, 1)
    ag_event()
    until((n2 + held[0][-1] + 1) // 2, NPA)
    for r in away + (0,):
        select(1, r, 0)
    ag_event()
    for r in away:
        go(gd_copy(0, r, 1))
    for r in range(PLANE):
        slot_grads(0, r, 0)
    until(n2 - 1, NPA - 1)
    me_copy(0, n2).wait_recv()
    for p in range(n2, nz):
        combine_rows(p)

    def rs_event(way, d, h):
        buf = fwd if way == 0 else bwd
        p = pos(d if way == 0 else -d)
        first = d == n2 or (d == n2 - 1 and h // (NPR // 2) != way)

        def body(i, _):
            at = pl.ds(pl.multiple_of(i * nt, nt), nt)
            tsum[way, :, at] = combine(p, h * rcut, rcut, at)
            return 0

        lax.fori_loop(0, width // nt, body, 0)
        if first:
            buf[d, h] = tsum[way].astype(BF)
        else:
            rs_copy(way, d + 1, h).wait_recv()
            buf[d, h] = (tsum[way] + buf[d, h].astype(F32)).astype(BF)
        go(rs_copy(way, d, h))

    def part_block(dy, rel):
        i = lax.rem(y + dy, ny) * 2 + flip(xh, rel)
        at = pl.ds(pl.multiple_of(i * db, db), db)
        part[dy, rel] = mm(dturn[...], xs[:, at]).astype(BF)
        if dy:
            go(py_copy(dy, rel))

    g_waited = set()

    def need(p):
        for w in parts_of(p):
            if (p // n2, w) not in g_waited:
                g_waited.add((p // n2, w))
                for r in range(1, PLANE):
                    gd_copy(p // n2, r, w).wait_recv()

    far = [dy for dy in (2, 1, 3) if dy < ny]

    def xd_wait():
        for c in range(2):
            for w in range(2):
                for r in range(1, PLANE):
                    xd_copy(c, r, w).wait_recv()

    def parts_away(rel):
        for dy in far:
            part_block(dy, rel)

    def parts_own():
        for rel in (1, 0):
            part_block(0, rel)

    def ysum(rel):
        total = part[0, rel].astype(F32)
        for dy in range(1, ny):
            total += prow[dy - 1, rel].astype(F32)
        return total

    def cross():
        for dy in range(1, ny):
            py_copy(dy, 1).wait_recv()
        xsend[...] = ysum(1).astype(BF)
        go(px)

    def last_rows():
        until(n2, NPA)
        for r in away + (0,):
            select(1, r, 1)
        for r in away:
            go(gd_copy(0, r, 0))

    steps = [(way, d, h) for d in range(n2, 0, -1) for h in range(NPR) for way in range(2) if d < n2 or h // (NPR // 2) == way]
    pairs = len(steps) // 2
    todo = [(1, last_rows), (pairs - 7, xd_wait), (pairs - 7, functools.partial(parts_away, 1)),
            (pairs - 6, functools.partial(parts_away, 0)), (pairs - 5, parts_own), (pairs - 2, cross)]
    for j in range(pairs):
        for way, d, h in steps[2 * j:2 * j + 2]:
            need(pos(d if way == 0 else -d))
            rs_event(way, d, h)
        while todo and todo[0][0] <= j:
            todo.pop(0)[1]()
    for _, what in todo:
        what()

    need(0)
    for h in range(NPR):
        for n in range(width // nt):
            at = slice(n * nt, (n + 1) * nt)
            tsum[h, :, at] = combine(0, h * rcut, rcut, at)
    for dy in range(1, ny):
        py_copy(dy, 0).wait_recv()
    px.wait_recv()
    total = (ysum(0) + xrow[...].astype(F32)).astype(BF)
    eye_d = jnp.where(
        lax.broadcasted_iota(I32, (db, db), 0) == lax.broadcasted_iota(I32, (db, db), 1), 1.0, 0.0
    ).astype(BF)
    turned = mm_nt(eye_d, total).astype(BF)
    gate_out[...] = turned[:, 0:ff]
    up_out[...] = turned[:, ff:2 * ff]
    for h in range(NPR):
        for way in range(2):
            rs_copy(way, 1, h).wait_recv()
        tok_out[h * rcut:(h + 1) * rcut] = (tsum[h] + fwd[0, h].astype(F32) + bwd[0, h].astype(F32)).astype(BF)
    for copy in started:
        copy.wait_send()


def hand_on(tok, gate, up, tok_out, gate_out, up_out):
    tok_out[...] = tok[...]
    gate_out[0] = gate[...]
    up_out[0] = up[...]


def on_device(nz, ny, tokens, expert_ids, keep_mask, gate_weights, hidden_grad, gate_pre, up_pre, gate_proj, up_proj):
    tdev, width = tokens.shape
    topk = expert_ids.shape[1]
    rows, ff = hidden_grad.shape[2:]
    cap = rows // (nz * PLANE)
    n2 = nz // 2
    ch = n2 * cap
    db = gate_proj.shape[1]
    dma = pltpu.SemaphoreType.DMA
    vm = pl.BlockSpec(memory_space=pltpu.VMEM)
    hbm = pl.BlockSpec(memory_space=pl.ANY)
    grads = jax.ShapeDtypeStruct((db, ff), BF)
    out = pl.pallas_call(
        functools.partial(kernel, nz, ny, cap, topk),
        out_shape=(jax.ShapeDtypeStruct((tdev, width), BF), grads, grads),
        in_specs=[vm] * 3 + [hbm] * 6,
        out_specs=(vm, vm, vm),
        scratch_shapes=[
            pltpu.VMEM((2, n2 * tdev, width), BF),
            pltpu.VMEM((nz, 2 * topk, tdev), F32),
            pltpu.VMEM((rows, 2 * ff), BF),
            pltpu.VMEM((rows, 2 * ff), BF),
            pltpu.VMEM((2 * ff, rows), BF),
            pltpu.VMEM((width, 2 * ff), BF),
            pltpu.VMEM((nz, tdev, PLANE * ch), BF),
            pltpu.VMEM((2, PLANE - 1, ch, width), BF),
            pltpu.VMEM((rows, width), BF),
            pltpu.VMEM((2, PLANE - 1, ch, width), BF),
            pltpu.VMEM((rows, width), BF),
            pltpu.VMEM((n2 + 1, NPR, tdev // NPR, width), BF),
            pltpu.VMEM((n2 + 1, NPR, tdev // NPR, width), BF),
            pltpu.VMEM((NPR, tdev // NPR, width), F32),
            pltpu.VMEM((ny, 2, 2 * ff, db), BF),
            pltpu.VMEM((max(ny - 1, 1), 2, 2 * ff, db), BF),
            pltpu.VMEM((2 * ff, db), BF),
            pltpu.VMEM((2 * ff, db), BF),
            dma((2, NPA * (n2 + 1))), dma((2, NPA * (n2 + 1))),
            dma((2, n2 + 1)), dma((2, n2 + 1)),
            dma((4, PLANE)), dma((4, PLANE)),
            dma((4, PLANE)), dma((4, PLANE)),
            dma, dma,
            dma((ny, 2)), dma((ny, 2)),
            dma((2, NPR * (n2 + 1))), dma((2, NPR * (n2 + 1))),
            dma((ny, 2)), dma((ny, 2)),
            dma, dma,
            pltpu.VMEM((rows, ff), BF),
            pltpu.VMEM((rows, ff), BF),
            pltpu.VMEM((rows, ff), BF),
            dma((6,)),
        ],
        compiler_params=pltpu.CompilerParams(
            collective_id=0, has_side_effects=True, vmem_limit_bytes=61000 * 1024
        ),
        cost_estimate=pl.CostEstimate(
            flops=2 * rows * width * ff * 4, bytes_accessed=6 * rows * ff + 4 * tdev * width, transcendentals=rows * ff
        ),
    )(
        expert_ids.T, keep_mask.T, gate_weights.T, tokens,
        hidden_grad[0, 0], gate_pre[0, 0], up_pre[0, 0], gate_proj[0], up_proj[0],
    )
    whole = jax.ShapeDtypeStruct((1, db, ff), BF)
    return pl.pallas_call(
        hand_on,
        out_shape=(jax.ShapeDtypeStruct((tdev, width), BF), whole, whole),
        in_specs=[vm] * 3,
        out_specs=(vm, vm, vm),
        cost_estimate=pl.CostEstimate(flops=0, bytes_accessed=4 * (tdev * width + 2 * db * ff), transcendentals=0),
    )(*out)


def solution(mesh):
    nz, ny = mesh.shape["expert"] // PLANE, mesh.shape["dp"] // 2
    both = P(("dp", "expert"), None)
    acts = P("dp", "expert", None, None)
    weights = P("expert", "dp", None)
    return jax.shard_map(
        functools.partial(on_device, nz, ny),
        mesh=mesh,
        in_specs=(both, both, both, both, acts, acts, acts, weights, weights),
        out_specs=(both, weights, weights),
        check_vma=False,
    )
```

```python
import functools

import jax
import jax.numpy as jnp
from jax import lax
from jax.experimental import pallas as pl
from jax.experimental.pallas import tpu as pltpu
from jax.sharding import PartitionSpec as P

MESH = pl.DeviceIdType.MESH
BF = jnp.bfloat16
F32 = jnp.float32
I32 = jnp.int32
NPA = 2
NPR = 2
PLANE = 4


def mm_nt(a, b):
    return lax.dot_general(a, b, (((1,), (1,)), ((), ())), preferred_element_type=F32)


def mm(a, b):
    return jnp.dot(a, b, preferred_element_type=F32)


def flip(bit, by):
    return bit + by - 2 * bit * by


def kernel(
    nz, ny, cap, topk,
    ids_in, keep_in, gate_in, tok, hid_in, pre_a_in, pre_b_in, w_gate, w_up,
    tok_out, gate_out, up_out,
    xcol, meta, delta, dperm, dturn, wall, st, xs_send, xs, g_send, g_all,
    fwd, bwd, tsum, part, prow, xsend, xrow,
    ag_s, ag_r, me_s, me_r, xd_s, xd_r, gd_s, gd_r, wx_s, wx_r, wy_s, wy_r,
    rs_s, rs_r, py_s, py_r, px_s, px_r, hid, pre_a, pre_b, in_s,
):
    n2 = nz // 2
    tdev, width = tok.shape
    cut, rcut = tdev // NPA, tdev // NPR
    ff = w_gate.shape[1]
    rows = hid.shape[0]
    ch = n2 * cap
    low = (n2 // 2) * cap // 16 * 16
    span = ((0, low), (low, ch - low))
    held = (range(0, -(-low // cap)), range(low // cap, n2))
    db = w_gate.shape[0]
    nt = min(512, width)
    e_ix, d_ix = lax.axis_index("expert"), lax.axis_index("dp")
    z, q = e_ix // PLANE, e_ix % PLANE
    xl, co = q // 2, q % 2
    y, xh = d_ix // 2, d_ix % 2
    zup = (d_ix, lax.rem(z + 1, nz) * PLANE + q)
    zdn = (d_ix, lax.rem(z + nz - 1, nz) * PLANE + q)
    column = [flip(xl, r // 2) * 2 + flip(co, r % 2) for r in range(PLANE)]
    plane = [(d_ix, z * PLANE + column[r]) for r in range(PLANE)]
    ypeer = [(lax.rem(y + dy, ny) * 2 + xh, e_ix) for dy in range(ny)]
    xpeer = (y * 2 + (1 - xh), e_ix)

    def pos(off):
        if off == -n2 or off == n2:
            return nz - 1
        return 2 * off if off >= 0 else -2 * off - 1

    def send(src, dst, s, r, dev):
        return pltpu.make_async_remote_copy(
            src_ref=src, dst_ref=dst, send_sem=s, recv_sem=r, device_id=dev, device_id_type=MESH
        )

    def slot_piece(p, h):
        return xcol.at[p // n2, pl.ds((p % n2) * tdev + h * cut, cut)]

    def ag_copy(way, d, h):
        sign = -1 if way == 0 else 1
        src = slot_piece(pos(sign * (d - 1)), h)
        ix = (way, d * NPA + h)
        return send(src, slot_piece(pos(sign * d), h), ag_s.at[ix], ag_r.at[ix], zup if way == 0 else zdn)

    def me_copy(way, d):
        sign = -1 if way == 0 else 1
        ix = (way, d)
        return send(meta.at[pos(sign * (d - 1))], meta.at[pos(sign * d)], me_s.at[ix], me_r.at[ix], zup if way == 0 else zdn)

    def xd_copy(c, r, w):
        at, n = span[w]
        ix = (c * 2 + w, r)
        return send(xs_send.at[c, r - 1, pl.ds(at, n)], xs.at[pl.ds((c * PLANE + r) * ch + at, n)], xd_s.at[ix], xd_r.at[ix], plane[r])

    def g_rows(c, w):
        return (c * ch + span[w][0]) * PLANE

    def gd_copy(c, r, w):
        at, n = span[w]
        ix = (c * 2 + w, r)
        return send(g_send.at[c, r - 1, pl.ds(at, n)], g_all.at[pl.ds(g_rows(c, w) + r * n, n)], gd_s.at[ix], gd_r.at[ix], plane[r])

    def wblock(i):
        return wall.at[pl.ds(pl.multiple_of(i * db, db), db)]

    wx = send(wblock(d_ix), wblock(d_ix), wx_s, wx_r, xpeer)

    def wy_copy(dy, rel):
        i = y * 2 + flip(xh, rel)
        return send(wblock(i), wblock(i), wy_s.at[dy, rel], wy_r.at[dy, rel], ypeer[dy])

    def wy_wait(dy, rel):
        i = lax.rem(y + ny - dy, ny) * 2 + flip(xh, rel)
        send(wblock(i), wblock(i), wy_s.at[dy, rel], wy_r.at[dy, rel], ypeer[dy]).wait_recv()

    def rs_copy(way, d, h):
        buf = fwd if way == 0 else bwd
        ix = (way, d * NPR + h)
        return send(buf.at[d, h], buf.at[d - 1, h], rs_s.at[ix], rs_r.at[ix], zup if way == 0 else zdn)

    def py_copy(dy, rel):
        return send(part.at[dy, rel], prow.at[dy - 1, rel], py_s.at[dy, rel], py_r.at[dy, rel], ypeer[dy])

    px = send(xsend, xrow, px_s, px_r, xpeer)
    started = []

    def go(copy):
        copy.start()
        started.append(copy)

    barrier = pltpu.get_barrier_semaphore()
    partners = [zup, zdn, xpeer] + plane[1:] + ypeer[1:]
    for dev in partners:
        pl.semaphore_signal(barrier, inc=1, device_id=dev, device_id_type=MESH)

    mine_w = pl.ds(pl.multiple_of(d_ix * db, db), db)
    fetch_w = [
        pltpu.make_async_copy(w_gate, wall.at[mine_w, pl.ds(0, ff)], in_s.at[0]),
        pltpu.make_async_copy(w_up, wall.at[mine_w, pl.ds(ff, ff)], in_s.at[1]),
    ]
    fetch = [
        pltpu.make_async_copy(hid_in, hid, in_s.at[2]),
        pltpu.make_async_copy(pre_a_in, pre_a, in_s.at[3]),
        pltpu.make_async_copy(pre_b_in, pre_b, in_s.at[4]),
        pltpu.make_async_copy(tok, xcol.at[0, pl.ds(0, tdev)], in_s.at[5]),
    ]
    for copy in fetch[3:] + fetch_w + fetch[:3]:
        copy.start()

    pl.semaphore_wait(barrier, len(partners))

    def ag_has(way, d, h):
        return d < n2 or (d == n2 and h // (NPA // 2) == way)

    def me_has(way, d):
        return d < n2 or (d == n2 and way == 0)

    fetch[3].wait()
    for way in range(2):
        if ag_has(way, 1, 0):
            go(ag_copy(way, 1, 0))

    experts = nz * PLANE
    ids, keep = ids_in[...], keep_in[...]
    e_iota = lax.broadcasted_iota(I32, (experts, tdev), 0)
    named = jnp.zeros((experts, tdev), F32)
    for k in range(topk):
        named += jnp.where((e_iota == ids[k:k + 1, :]) & (keep[k:k + 1, :] > 0), 1.0, 0.0)
    earlier = jnp.where(
        lax.broadcasted_iota(I32, (tdev, tdev), 0) < lax.broadcasted_iota(I32, (tdev, tdev), 1), 1.0, 0.0
    ).astype(BF)
    before = mm(named.astype(BF), earlier)
    for k in range(topk):
        mine = ids[k:k + 1, :]
        slot = jnp.sum(jnp.where(e_iota == mine, before, 0.0), axis=0, keepdims=True)
        row = mine.astype(F32) * float(cap) + slot
        meta[0, k:k + 1, :] = jnp.where(keep[k:k + 1, :] > 0, row, -4096.0)
    meta[0, topk:2 * topk, :] = gate_in[...].astype(F32)

    for way in range(2):
        go(me_copy(way, 1))
    for h in range(1, NPA):
        for way in range(2):
            if ag_has(way, 1, h):
                go(ag_copy(way, 1, h))
    for copy in fetch_w:
        copy.wait()
    go(wx)
    for dy in range(1, ny):
        go(wy_copy(dy, 0))

    events = [(d, h) for d in range(1, n2) for h in range(NPA)] + [(n2, h) for h in range(NPA // 2)]
    queue = list(events)

    def ag_event():
        if not queue:
            return
        d, h = queue.pop(0)
        for way in range(2):
            if h == 0 and me_has(way, d) and d < n2:
                me_copy(way, d).wait_recv()
                if me_has(way, d + 1):
                    go(me_copy(way, d + 1))
        for way in range(2):
            hh = h + way * (NPA // 2) if d == n2 else h
            ag_copy(way, d, hh).wait_recv()
            if ag_has(way, d + 1, hh):
                go(ag_copy(way, d + 1, hh))

    tile = 96 if rows % 96 == 0 else rows
    tiles = rows // tile

    def delta_tile(i, _):
        at = pl.ds(pl.multiple_of(i * tile, tile), tile)
        a, b, dh = pre_a[at].astype(F32), pre_b[at].astype(F32), hid[at].astype(F32)
        s = 1.0 / (1.0 + jnp.exp(-a))
        delta[at, 0:ff] = (dh * b * s * (1.0 + a * (1.0 - s))).astype(BF)
        delta[at, ff:2 * ff] = (dh * a * s).astype(BF)
        return 0

    def perm_block(i, _):
        c, r = i // PLANE, i % PLANE
        other = flip(xl, r // 2) * 2 + flip(co, r % 2)
        rr = lax.broadcasted_iota(I32, (ch, 1), 0)
        m = jnp.zeros((ch, 1), I32)
        for k in range(1, n2):
            m += jnp.where(rr >= k * cap, 1, 0)
        p = m + c * n2
        low = p & 1
        off = jnp.where(low == 0, p >> 1, -((p + 1) >> 1))
        zz = off + z
        zz = jnp.where(zz < 0, zz + nz, zz)
        zz = jnp.where(zz >= nz, zz - nz, zz)
        want = zz * (PLANE * cap) + other * cap + rr - m * cap
        pick = jnp.where(lax.broadcasted_iota(I32, (ch, rows), 1) == want, 1.0, 0.0).astype(BF)
        dperm[pl.ds(pl.multiple_of(i * ch, ch), ch)] = mm(pick, delta[...]).astype(BF)
        return 0

    def turn_block(i, _):
        eye = jnp.where(
            lax.broadcasted_iota(I32, (128, 2 * ff), 0) + i * 128 == lax.broadcasted_iota(I32, (128, 2 * ff), 1), 1.0, 0.0
        ).astype(BF)
        dturn[pl.ds(pl.multiple_of(i * 128, 128), 128)] = mm_nt(eye, dperm[...]).astype(BF)
        return 0

    turns = 2 * ff // 128

    def pick_rows(p, r, w):
        base = ((z * PLANE + column[r]) * cap).astype(F32)
        v = meta[p, 0:topk, :] - base
        valid = (v >= 0.0) & (v < float(cap))
        row = jnp.max(jnp.where(valid, v + float((p % n2) * cap - span[w][0]), -1.0), axis=0, keepdims=True)
        weight = jnp.sum(jnp.where(valid, meta[p, topk:2 * topk, :], 0.0), axis=0, keepdims=True)
        it = lax.broadcasted_iota(I32, (span[w][1], tdev), 0).astype(F32)
        return jnp.where(it == row, weight, 0.0).astype(BF)

    eye_t = jnp.where(
        lax.broadcasted_iota(I32, (tdev, tdev), 0) == lax.broadcasted_iota(I32, (tdev, tdev), 1), 1.0, 0.0
    ).astype(BF)

    def parts_of(p):
        return [w for w in range(2) if p % n2 in held[w]]

    def columns_of(w):
        return slice(span[w][0] * PLANE, (span[w][0] + span[w][1]) * PLANE)

    def combine_rows(p):
        for w in parts_of(p):
            s = jnp.concatenate([pick_rows(p, r, w) for r in range(PLANE)], axis=0)
            st[p, :, columns_of(w)] = mm_nt(eye_t, s).astype(BF)

    def combine(p, lo, n, at):
        c = p // n2
        total = None
        for w in parts_of(p):
            one = mm(st[p, lo:lo + n, columns_of(w)], g_all[pl.ds(g_rows(c, w), span[w][1] * PLANE), at])
            total = one if total is None else total + one
        return total

    def select(c, r, w):
        first, n = span[w]
        s = jnp.concatenate([pick_rows(c * n2 + m, r, w) for m in held[w]], axis=1)
        src = slice(held[w][0] * tdev, (held[w][-1] + 1) * tdev)

        def body(i, _):
            at = pl.ds(pl.multiple_of(i * nt, nt), nt)
            got = mm(s, xcol[c, src, at]).astype(BF)
            if r == 0:
                xs[pl.ds(c * PLANE * ch + first, n), at] = got
            else:
                xs_send[c, r - 1, first:first + n, at] = got
            return 0

        lax.fori_loop(0, width // nt, body, 0)
        if r:
            go(xd_copy(c, r, w))

    def slot_grads(c, r, w):
        first, n = span[w]
        lhs = dperm[pl.ds((c * PLANE + r) * ch + first, n)]

        def body(i, _):
            at = pl.ds(pl.multiple_of(i * nt, nt), nt)
            got = mm_nt(lhs, wall[at]).astype(BF)
            if r == 0:
                g_all[pl.ds(g_rows(c, w), n), at] = got
            else:
                g_send[c, r - 1, first:first + n, at] = got
            return 0

        lax.fori_loop(0, width // nt, body, 0)

    def until(d, h):
        while queue and queue[0] <= (d, h):
            ag_event()

    away = (2, 3, 1)

    for copy in fetch[:3]:
        copy.wait()
    lax.fori_loop(0, tiles, delta_tile, 0)
    ag_event()
    lax.fori_loop(PLANE, 2 * PLANE, perm_block, 0)
    ag_event()
    wx_i = y * 2 + (1 - xh)
    send(wblock(wx_i), wblock(wx_i), wx_s, wx_r, xpeer).wait_recv()
    for dy in range(1, ny):
        go(wy_copy(dy, 1))
    lax.fori_loop(0, PLANE, perm_block, 0)
    ag_event()
    lax.fori_loop(0, turns, turn_block, 0)
    until((held[0][-1] + 1) // 2, NPA)
    for r in away + (0,):
        select(0, r, 0)
    ag_event()
    for p in range(n2 // 2):
        combine_rows(p)
    ag_event()
    for dy in range(1, ny):
        for rel in range(2):
            wy_wait(dy, rel)
    for r in away:
        slot_grads(1, r, 1)
        go(gd_copy(1, r, 1))
    ag_event()
    slot_grads(1, 0, 1)
    until(n2 // 2, NPA)
    for r in away:
        select(0, r, 1)
    for r in away:
        slot_grads(1, r, 0)
        go(gd_copy(1, r, 0))
    ag_event()
    select(0, 0, 1)
    slot_grads(1, 0, 0)
    for p in range(n2 // 2, n2):
        combine_rows(p)
    ag_event()
    for r in range(PLANE):
        slot_grads(0, r, 1)
    ag_event()
    until((n2 + held[0][-1] + 1) // 2, NPA)
    for r in away + (0,):
        select(1, r, 0)
    ag_event()
    for r in away:
        go(gd_copy(0, r, 1))
    for r in range(PLANE):
        slot_grads(0, r, 0)
    until(n2 - 1, NPA - 1)
    me_copy(0, n2).wait_recv()
    for p in range(n2, nz):
        combine_rows(p)

    def rs_event(way, d, h):
        buf = fwd if way == 0 else bwd
        p = pos(d if way == 0 else -d)
        first = d == n2 or (d == n2 - 1 and h // (NPR // 2) != way)

        def body(i, _):
            at = pl.ds(pl.multiple_of(i * nt, nt), nt)
            tsum[way, :, at] = combine(p, h * rcut, rcut, at)
            return 0

        lax.fori_loop(0, width // nt, body, 0)
        if first:
            buf[d, h] = tsum[way].astype(BF)
        else:
            rs_copy(way, d + 1, h).wait_recv()
            buf[d, h] = (tsum[way] + buf[d, h].astype(F32)).astype(BF)
        go(rs_copy(way, d, h))

    def part_block(dy, rel):
        i = lax.rem(y + dy, ny) * 2 + flip(xh, rel)
        at = pl.ds(pl.multiple_of(i * db, db), db)
        part[dy, rel] = mm(dturn[...], xs[:, at]).astype(BF)
        if dy:
            go(py_copy(dy, rel))

    g_waited = set()

    def need(p):
        for w in parts_of(p):
            if (p // n2, w) not in g_waited:
                g_waited.add((p // n2, w))
                for r in range(1, PLANE):
                    gd_copy(p // n2, r, w).wait_recv()

    far = [dy for dy in (2, 1, 3) if dy < ny]

    def xd_wait():
        for c in range(2):
            for w in range(2):
                for r in range(1, PLANE):
                    xd_copy(c, r, w).wait_recv()

    def parts_away(rel):
        for dy in far:
            part_block(dy, rel)

    def parts_own():
        for rel in (1, 0):
            part_block(0, rel)

    def ysum(rel):
        total = part[0, rel].astype(F32)
        for dy in range(1, ny):
            total += prow[dy - 1, rel].astype(F32)
        return total

    def cross():
        for dy in range(1, ny):
            py_copy(dy, 1).wait_recv()
        xsend[...] = ysum(1).astype(BF)
        go(px)

    def last_rows():
        until(n2, NPA)
        for r in away + (0,):
            select(1, r, 1)
        for r in away:
            go(gd_copy(0, r, 0))

    steps = [(way, d, h) for d in range(n2, 0, -1) for h in range(NPR) for way in range(2) if d < n2 or h // (NPR // 2) == way]
    pairs = len(steps) // 2
    todo = [(1, last_rows), (pairs - 7, xd_wait), (pairs - 7, functools.partial(parts_away, 1)),
            (pairs - 6, functools.partial(parts_away, 0)), (pairs - 5, parts_own), (pairs - 2, cross)]
    for j in range(pairs):
        for way, d, h in steps[2 * j:2 * j + 2]:
            need(pos(d if way == 0 else -d))
            rs_event(way, d, h)
        while todo and todo[0][0] <= j:
            todo.pop(0)[1]()
    for _, what in todo:
        what()

    need(0)
    for h in range(NPR):
        for n in range(width // nt):
            at = slice(n * nt, (n + 1) * nt)
            tsum[h, :, at] = combine(0, h * rcut, rcut, at)
    for dy in range(1, ny):
        py_copy(dy, 0).wait_recv()
    px.wait_recv()
    total = (ysum(0) + xrow[...].astype(F32)).astype(BF)
    eye_d = jnp.where(
        lax.broadcasted_iota(I32, (db, db), 0) == lax.broadcasted_iota(I32, (db, db), 1), 1.0, 0.0
    ).astype(BF)
    turned = mm_nt(eye_d, total).astype(BF)
    gate_out[...] = turned[:, 0:ff]
    up_out[...] = turned[:, ff:2 * ff]
    for h in range(NPR):
        for way in range(2):
            rs_copy(way, 1, h).wait_recv()
        tok_out[h * rcut:(h + 1) * rcut] = (tsum[h] + fwd[0, h].astype(F32) + bwd[0, h].astype(F32)).astype(BF)
    for copy in started:
        copy.wait_send()


def hand_on(tok, gate, up, tok_out, gate_out, up_out):
    tok_out[...] = tok[...]
    gate_out[0] = gate[...]
    up_out[0] = up[...]


def on_device(nz, ny, tokens, expert_ids, keep_mask, gate_weights, hidden_grad, gate_pre, up_pre, gate_proj, up_proj):
    tdev, width = tokens.shape
    topk = expert_ids.shape[1]
    rows, ff = hidden_grad.shape[2:]
    cap = rows // (nz * PLANE)
    n2 = nz // 2
    ch = n2 * cap
    db = gate_proj.shape[1]
    dma = pltpu.SemaphoreType.DMA
    vm = pl.BlockSpec(memory_space=pltpu.VMEM)
    hbm = pl.BlockSpec(memory_space=pl.ANY)
    grads = jax.ShapeDtypeStruct((db, ff), BF)
    out = pl.pallas_call(
        functools.partial(kernel, nz, ny, cap, topk),
        out_shape=(jax.ShapeDtypeStruct((tdev, width), BF), grads, grads),
        in_specs=[vm] * 3 + [hbm] * 6,
        out_specs=(vm, vm, vm),
        scratch_shapes=[
            pltpu.VMEM((2, n2 * tdev, width), BF),
            pltpu.VMEM((nz, 2 * topk, tdev), F32),
            pltpu.VMEM((rows, 2 * ff), BF),
            pltpu.VMEM((rows, 2 * ff), BF),
            pltpu.VMEM((2 * ff, rows), BF),
            pltpu.VMEM((width, 2 * ff), BF),
            pltpu.VMEM((nz, tdev, PLANE * ch), BF),
            pltpu.VMEM((2, PLANE - 1, ch, width), BF),
            pltpu.VMEM((rows, width), BF),
            pltpu.VMEM((2, PLANE - 1, ch, width), BF),
            pltpu.VMEM((rows, width), BF),
            pltpu.VMEM((n2 + 1, NPR, tdev // NPR, width), BF),
            pltpu.VMEM((n2 + 1, NPR, tdev // NPR, width), BF),
            pltpu.VMEM((NPR, tdev // NPR, width), F32),
            pltpu.VMEM((ny, 2, 2 * ff, db), BF),
            pltpu.VMEM((max(ny - 1, 1), 2, 2 * ff, db), BF),
            pltpu.VMEM((2 * ff, db), BF),
            pltpu.VMEM((2 * ff, db), BF),
            dma((2, NPA * (n2 + 1))), dma((2, NPA * (n2 + 1))),
            dma((2, n2 + 1)), dma((2, n2 + 1)),
            dma((4, PLANE)), dma((4, PLANE)),
            dma((4, PLANE)), dma((4, PLANE)),
            dma, dma,
            dma((ny, 2)), dma((ny, 2)),
            dma((2, NPR * (n2 + 1))), dma((2, NPR * (n2 + 1))),
            dma((ny, 2)), dma((ny, 2)),
            dma, dma,
            pltpu.VMEM((rows, ff), BF),
            pltpu.VMEM((rows, ff), BF),
            pltpu.VMEM((rows, ff), BF),
            dma((6,)),
        ],
        compiler_params=pltpu.CompilerParams(
            collective_id=0, has_side_effects=True, vmem_limit_bytes=61000 * 1024
        ),
        cost_estimate=pl.CostEstimate(
            flops=2 * rows * width * ff * 4, bytes_accessed=6 * rows * ff + 4 * tdev * width, transcendentals=rows * ff
        ),
    )(
        expert_ids.T, keep_mask.T, gate_weights.T, tokens,
        hidden_grad[0, 0], gate_pre[0, 0], up_pre[0, 0], gate_proj[0], up_proj[0],
    )
    whole = jax.ShapeDtypeStruct((1, db, ff), BF)
    return pl.pallas_call(
        hand_on,
        out_shape=(jax.ShapeDtypeStruct((tdev, width), BF), whole, whole),
        in_specs=[vm] * 3,
        out_specs=(vm, vm, vm),
        cost_estimate=pl.CostEstimate(flops=0, bytes_accessed=4 * (tdev * width + 2 * db * ff), transcendentals=0),
    )(*out)


def solution(mesh):
    nz, ny = mesh.shape["expert"] // PLANE, mesh.shape["dp"] // 2
    both = P(("dp", "expert"), None)
    acts = P("dp", "expert", None, None)
    weights = P("expert", "dp", None)
    return jax.shard_map(
        functools.partial(on_device, nz, ny),
        mesh=mesh,
        in_specs=(both, both, both, both, acts, acts, acts, weights, weights),
        out_specs=(both, weights, weights),
        check_vma=False,
    )
```
